512 devices in a mesh: cfg: 2 (over core), pipe: 4 (over x), seq: 64 (over y, z).
Axes of the slice: x: 4, y: 8, z: 8, core: 2. Of those that a mesh axis runs over, the one named last changes fastest.
Arguments:
- latent: bfloat16 [4, 512, 2048], P(None, 'seq'), may hold values from -6 to 6
- modulation: float32 [4, 2, 3, 2048], P('pipe', 'cfg'), may hold values from -4 to 4
- qkv_weight: bfloat16 [4, 2048, 6144], P('pipe', None, 'seq'), may hold values from -0.125 to 0.125
- out_weight: bfloat16 [4, 2048, 2048], P('pipe', 'seq'), may hold values from -0.125 to 0.125
- norm_gain: float32 [4, 2, 128], P('pipe'), may hold values from 1.2 to 2
- stale_kv: bfloat16 [4, 2, 2, 4, 64, 8, 8, 256], P('pipe', 'cfg', None, None, 'seq'), may hold values from -2 to 2
Outputs:
- guided: bfloat16 [4, 512, 2048], P('pipe', 'seq', 'cfg')
- next_kv: bfloat16 [4, 2, 2, 4, 64, 8, 8, 256], P('pipe', 'cfg', None, None, 'seq')
The draws below stay inside these ranges and needn't reach their ends.
All inputs are finite; a program needn't handle non-finite values.
Results may differ from the reference program's by a relative error of at most 0.033.
Values may be sent and summed in bfloat16 or wider, within the bound.
A program may use at most 64 MiB of HBM per device.

```python
import math
import jax
import jax.numpy as jnp
from jax import lax

HEAD_DIM = 128
HEADS = 16
D = 2048
TOK_DEV = 8
PATCHES = 4
TOKP = 512
SLICES = 8
MEMBERS = 8
HEAD_LOCAL = 2
N_PIPE = 4
N_SEQ = 64


def block_scale(key, extent, cuts, low, top_value):
    gain = 1.0
    for axis_at, blocks in cuts:
        steps = jax.random.uniform(jax.random.fold_in(jax.random.fold_in(key, 6), axis_at), (blocks,), jnp.float32, low / len(cuts), top_value / len(cuts))
        gain = gain * jnp.repeat(jnp.exp(steps), extent[axis_at] // blocks).reshape((-1,) + (1,) * (len(extent) - 1 - axis_at))
    return gain


def normal_values(rng, shape, deviation, limit, cuts=(), kind=jnp.bfloat16):
    drawn = jax.random.normal(rng, shape, jnp.float32) * deviation
    if len(cuts) > 0:
        drawn = block_scale(rng, shape, cuts, -0.22, 0.18) * drawn
    return jnp.clip(drawn, min=-limit, max=limit).astype(kind)


def setup_inputs(seed: int = 0) -> dict:
    streams_of = jax.random.split(jax.random.key(seed), 7)
    latent = normal_values(streams_of[0], (PATCHES, TOKP, D), 1.0, 6.0, ((1, 64),))
    modulation = normal_values(streams_of[1], (N_PIPE, 2, 3, D), 1.0, 4.0, ((0, 4), (1, 2)), jnp.float32)
    qkv_weight = normal_values(streams_of[2], (N_PIPE, D, 3 * D), D ** -0.5, 0.125, ((0, 4), (2, 64)))
    out_weight = normal_values(streams_of[3], (N_PIPE, D, D), D ** -0.5, 0.125, ((0, 4), (1, 64)))
    norm_gain = jnp.clip(1.2 + 0.79999995 * jax.random.uniform(streams_of[4], (N_PIPE, 2, HEAD_DIM), jnp.float32) ** block_scale(streams_of[4], (N_PIPE, 2, HEAD_DIM), ((0, 4),), -0.2, 0.2), 1.2, 2.0)
    stale_kv = jnp.clip(jax.random.uniform(streams_of[5], (N_PIPE, 2, 2, PATCHES, N_SEQ, SLICES, TOK_DEV, HEAD_LOCAL * HEAD_DIM), jnp.float32, -2.0, 2.0) * block_scale(streams_of[5], (N_PIPE, 2, 2, PATCHES, N_SEQ, SLICES, TOK_DEV, HEAD_LOCAL * HEAD_DIM), ((0, 4), (1, 2), (4, 64)), -0.4, 0.0), -2.0, 2.0).astype(jnp.bfloat16)
    return dict(latent=latent, modulation=modulation, qkv_weight=qkv_weight, out_weight=out_weight, norm_gain=norm_gain, stale_kv=stale_kv)


GUIDANCE_SCALE = 6.0
EPSILON = 1e-06

def layer_norm(values):
    center = values - lax.optimization_barrier(jnp.mean(values, axis=-1, keepdims=True))
    spread = lax.optimization_barrier(jnp.mean(center * center, axis=-1, keepdims=True))
    return center * lax.rsqrt(spread + EPSILON)

def head_norm(values, gain_row):
    return values * lax.rsqrt(lax.optimization_barrier(jnp.mean(values * values, axis=-1, keepdims=True)) + EPSILON) * gain_row

def attend(queries, key_rows, value_rows):

    def one_head(operands):
        query_head, key_head, value_head = operands
        scores = jnp.dot(query_head, key_head.T, preferred_element_type=jnp.float32) / math.sqrt(HEAD_DIM)
        weights = jnp.exp(scores)
        weight_total = lax.optimization_barrier(jnp.sum(weights, axis=-1, keepdims=True))
        summed = jnp.dot(weights.astype(jnp.bfloat16), value_head, preferred_element_type=jnp.float32)
        return (summed / weight_total).astype(jnp.bfloat16)
    return lax.map(one_head, (queries, key_rows, value_rows))

def reference(latent, modulation, qkv_weight, out_weight, norm_gain, stale_kv):
    stored = stale_kv.reshape(N_PIPE, 2, 2, PATCHES, SLICES, MEMBERS, SLICES, TOK_DEV, HEAD_LOCAL, HEAD_DIM)
    stored = stored.transpose(0, 1, 2, 3, 6, 5, 7, 4, 8, 9).reshape(N_PIPE, 2, 2, PATCHES, TOKP, HEADS, HEAD_DIM)
    member_of = jnp.arange(TOKP, dtype=jnp.int32) // TOK_DEV % MEMBERS
    patch_ids = jnp.arange(PATCHES, dtype=jnp.int32)
    finals = []
    kept_caches = []
    for branch in range(2):
        carried = [latent[patch_index] for patch_index in range(PATCHES)]
        section_caches = []
        for section_index in range(N_PIPE):
            shift_row = modulation[section_index, branch, 0]
            scale_row = modulation[section_index, branch, 1]
            gate_row = modulation[section_index, branch, 2]
            stale_keys = stored[section_index, branch, 0]
            stale_values = stored[section_index, branch, 1]
            fresh_keys = stale_keys
            fresh_values = stale_values
            for patch_index in range(PATCHES):
                hidden_in = carried[patch_index]
                normed = layer_norm(hidden_in.astype(jnp.float32))
                modulated = (normed * (1.0 + scale_row) + shift_row).astype(jnp.bfloat16)
                mixed = jnp.dot(modulated, qkv_weight[section_index], preferred_element_type=jnp.float32)
                mixed = mixed.reshape(TOKP, HEADS, 3, HEAD_DIM)
                queries = head_norm(mixed[:, :, 0], norm_gain[section_index, 0]).astype(jnp.bfloat16)
                new_keys = head_norm(mixed[:, :, 1], norm_gain[section_index, 1]).astype(jnp.bfloat16)
                new_values = mixed[:, :, 2].astype(jnp.bfloat16)
                fresh_keys = fresh_keys.at[patch_index].set(new_keys)
                fresh_values = fresh_values.at[patch_index].set(new_values)
                grouped = queries.reshape(SLICES, MEMBERS, TOK_DEV, HEADS, HEAD_DIM)
                pieces = []
                for member in range(MEMBERS):
                    use_fresh = jnp.logical_and(patch_ids[:, None] <= patch_index, member_of[None, :] == member)
                    key_view = jnp.where(use_fresh[:, :, None, None], fresh_keys, stale_keys)
                    value_view = jnp.where(use_fresh[:, :, None, None], fresh_values, stale_values)
                    key_view = key_view.reshape(PATCHES * TOKP, HEADS, HEAD_DIM).transpose(1, 0, 2)
                    value_view = value_view.reshape(PATCHES * TOKP, HEADS, HEAD_DIM).transpose(1, 0, 2)
                    rows = grouped[:, member].reshape(SLICES * TOK_DEV, HEADS, HEAD_DIM).transpose(1, 0, 2)
                    attended_rows = attend(rows, key_view, value_view)
                    pieces.append(attended_rows.transpose(1, 0, 2).reshape(SLICES, TOK_DEV, D))
                attended = jnp.stack(pieces, axis=1).reshape(TOKP, D)
                projected = jnp.dot(attended, out_weight[section_index], preferred_element_type=jnp.float32)
                carried[patch_index] = (hidden_in.astype(jnp.float32) + gate_row * projected).astype(jnp.bfloat16)
            section_caches.append(jnp.stack((fresh_keys, fresh_values)))
        finals.append(jnp.stack(carried))
        kept_caches.append(jnp.stack(section_caches))
    conditional = finals[0].astype(jnp.float32)
    unconditional = finals[1].astype(jnp.float32)
    guided = (unconditional + GUIDANCE_SCALE * (conditional - unconditional)).astype(jnp.bfloat16)
    next_kv = jnp.stack(kept_caches).transpose(1, 0, 2, 3, 4, 5, 6)
    next_kv = next_kv.reshape(N_PIPE, 2, 2, PATCHES, SLICES, MEMBERS, TOK_DEV, SLICES, HEAD_LOCAL, HEAD_DIM)
    next_kv = next_kv.transpose(0, 1, 2, 3, 7, 5, 4, 6, 8, 9)
    next_kv = next_kv.reshape(N_PIPE, 2, 2, PATCHES, N_SEQ, SLICES, TOK_DEV, HEAD_LOCAL * HEAD_DIM)
    return (guided, next_kv)
```

```python
import functools
import math

import jax
import jax.numpy as jnp
from jax import lax
from jax.experimental import pallas as pl
from jax.experimental.pallas import tpu as pltpu
from jax.sharding import PartitionSpec as P

GUIDANCE_SCALE = 6.0
EPSILON = 1e-06
MESH = pl.DeviceIdType.MESH
F32 = jnp.float32
BF16 = jnp.bfloat16
NT = (((1,), (1,)), ((), ()))


def packed_rows(values):
    half = values.shape[-1] // 2
    return jnp.concatenate((values[..., :half], values[..., half:]), axis=-2)


def head_norm(values, gain_row):
    square = jnp.mean(values * values, axis=-1, keepdims=True)
    return values * lax.rsqrt(square + EPSILON) * gain_row


def kernel(
    sizes,
    latent,
    modulation,
    qkv_piece,
    out_piece,
    gains,
    stale,
    guided_out,
    own_kv,
    qkv_all,
    out_all,
    others,
    inputs,
    features,
    mixed_left,
    partials,
    arrived,
    finals,
    partner,
    guided_sent,
    z_send,
    z_recv,
    pair_send,
    pair_recv,
    gather_send,
    gather_recv,
    scatter_send,
    scatter_recv,
    pipe_send,
    pipe_recv,
    cfg_send,
    cfg_recv,
    guided_send,
    guided_recv,
):
    sections, slices, members, patches = sizes
    branch = lax.axis_index("cfg")
    section = lax.axis_index("pipe")
    rank = lax.axis_index("seq")
    y = rank // members
    z = rank % members
    rows = features.shape[1] * 8
    width = features.shape[3]
    middle = members // 2

    def at_y(index):
        return (branch, section, index * members + z)

    def at_z(index):
        return (branch, section, y * members + index)

    right = at_z((z + 1) % members)
    left = at_z((z + members - 1) % members)
    sibling = (1 - branch, section, rank)

    def at_pipe(index):
        return (branch, index, rank)

    barrier = pltpu.get_barrier_semaphore()
    greeted = [at_y((y + d) % slices) for d in range(1, slices)]
    greeted += [right, left, sibling]
    greeted += [at_pipe((section + d) % sections) for d in range(1, sections)]
    for device in greeted:
        pl.semaphore_signal(barrier, inc=1, device_id=device, device_id_type=MESH)
    pl.semaphore_wait(barrier, len(greeted))

    def remote(src, dst, send, recv, device):
        return pltpu.make_async_remote_copy(
            src_ref=src,
            dst_ref=dst,
            send_sem=send,
            recv_sem=recv,
            device_id=device,
            device_id_type=MESH,
        )

    def part(ref, step, way):
        if step < middle:
            return ref
        return ref.at[:, pl.ds(way * 1024, 1024)]

    def hop(step, way, item, lands=False):
        device = left if way else right
        sign = 1 if way else members - 1
        owner = (z + sign * (step - 1)) % members
        block = (z + sign * step) % members if lands else owner
        send, recv = z_send.at[item, way, step - 1], z_recv.at[item, way, step - 1]
        if item == 2:
            source = (step - 1 if way == 0 else members - step + 1) - 1
            target = (step if way == 0 else members - step) - 1
            here = stale if step == 1 else others.at[source]
            there = others.at[target]
            if step == middle:
                here, there = here.at[way], there.at[way]
        else:
            piece, full = (qkv_piece, qkv_all) if item == 0 else (out_piece, out_all)
            here = piece.at[branch] if step == 1 else full.at[owner * 2 + branch]
            here = part(here, step, way)
            there = part(full.at[block * 2 + branch], step, way)
        return remote(here, there, send, recv, device)

    def handed(step, way, item, lands=False):
        sign = 1 if way else members - 1
        landing = (z + sign * step) % members
        full = qkv_all if item == 0 else out_all
        send, recv = pair_send.at[item, way, step - 1], pair_recv.at[item, way, step - 1]
        half = 1 - branch if lands else branch
        block = part(full.at[landing * 2 + half], step, way)
        return remote(block, block, send, recv, sibling)

    for item in (0, 2, 1):
        for way in (0, 1):
            hop(1, way, item).start()

    for half in (0, 1):
        qkv_all[z * 2 + half] = qkv_piece[half]
        out_all[z * 2 + half] = out_piece[half]
    own_kv[...] = stale[...]

    @pl.when(section == 0)
    def _():
        inputs[...] = latent[...]

    for step in range(1, middle + 1):
        for item in (0, 2, 1):
            for way in (0, 1):
                hop(step, way, item, lands=True).wait_recv()
                if step < middle:
                    hop(step + 1, way, item).start()
                if item != 2:
                    handed(step, way, item).start()
    for step in range(1, middle + 1):
        for item in (0, 1):
            for way in (0, 1):
                handed(step, way, item, lands=True).wait_recv()

    order = [4, 3, 5, 2, 6, 1, 7] if slices == 8 else list(range(1, slices))

    def gather_copy(p, d):
        return remote(
            features.at[p, y],
            features.at[p, y],
            gather_send.at[p, d],
            gather_recv.at[p, d],
            at_y((y + d) % slices),
        )

    def gather_landing(p, d):
        return remote(
            features.at[p, y],
            features.at[p, (y + slices - d) % slices],
            gather_send.at[p, d],
            gather_recv.at[p, d],
            at_y((y + d) % slices),
        )

    def scatter_copy(p, d):
        return remote(
            partials.at[p, (y + d) % slices],
            arrived.at[p, d],
            scatter_send.at[p, d],
            scatter_recv.at[p, d],
            at_y((y + d) % slices),
        )

    def pipe_copy(p):
        return remote(
            finals.at[p],
            inputs.at[p],
            pipe_send.at[p],
            pipe_recv.at[p],
            at_pipe((section + 1) % sections),
        )

    def cfg_copy(p):
        return remote(finals.at[p], partner.at[p], cfg_send.at[p], cfg_recv.at[p], sibling)

    def both(left_rows):
        total = left_rows[:8] + left_rows[8:]
        return jnp.concatenate((total, total), axis=0)

    def start_patch(p):
        @pl.when(section > 0)
        def _():
            pipe_copy(p).wait_recv()

        x = inputs[p].astype(F32)
        count = 2 * width
        center = x - both(jnp.sum(x, axis=1, keepdims=True)) / count
        spread = both(jnp.sum(center * center, axis=1, keepdims=True)) / count
        normed = center * lax.rsqrt(spread + EPSILON)
        features[p, y] = (normed * (1.0 + modulation[1]) + modulation[0]).astype(BF16)
        for d in order:
            gather_copy(p, d).start()

    def attend(p):
        for d in order:
            gather_landing(p, d).wait_recv()
        stacked = features[p].astype(F32)
        mixed_left[0] = stacked[:, :8].reshape(rows, width).astype(BF16)
        mixed_left[1] = stacked[:, 8:].reshape(rows, width).astype(BF16)
        sums = []
        for head in range(2):
            total = None
            for piece in range(4):
                side, lane = piece // 2, (piece % 2) * 512
                weight = qkv_all[pl.ds(head * members, members), :, pl.ds(piece * 512, 512)]
                product = lax.dot_general(
                    mixed_left[side, :, pl.ds(lane, 512)],
                    weight.reshape(members * weight.shape[1], 512),
                    NT,
                    preferred_element_type=F32,
                )
                total = product if total is None else total + product
            sums.append(total)
        queries = [head_norm(m[:, :128], gains[0:1]).astype(BF16) for m in sums]
        keys = [head_norm(m[:, 128:256], gains[1:2]).astype(BF16) for m in sums]
        values = [m[:, 256:].astype(BF16) for m in sums]
        own_kv[0, p] = jnp.concatenate(keys, axis=1)
        own_kv[1, p] = jnp.concatenate(values, axis=1)
        attended = []
        scale = 1.0 / math.sqrt(128)
        for head in range(2):
            lanes = pl.ds(head * 128, 128)
            summed, weight_sum = None, None
            for member in range(members):
                block = own_kv if member == members - 1 else others.at[member]
                key_rows = block[0, :, :, lanes].reshape(patches * rows, 128)
                value_rows = block[1, :, :, lanes].reshape(patches * rows, 128)
                scores = lax.dot_general(
                    queries[head], key_rows, NT, preferred_element_type=F32
                )
                weights = jnp.exp(scores * scale)
                product = jnp.dot(
                    weights.astype(BF16), value_rows, preferred_element_type=F32
                )
                summed = product if summed is None else summed + product
                weight_sum = weights if weight_sum is None else weight_sum + weights
            attended.append(
                (summed / jnp.sum(weight_sum, axis=1, keepdims=True)).astype(BF16)
            )
        attended = jnp.concatenate(attended, axis=1)
        out_rows = members * 32
        for lane in range(0, width, 512):
            low = jnp.dot(
                attended,
                out_all[:, :, pl.ds(lane, 512)].reshape(out_rows, 512),
                preferred_element_type=F32,
            )
            high = jnp.dot(
                attended,
                out_all[:, :, pl.ds(width + lane, 512)].reshape(out_rows, 512),
                preferred_element_type=F32,
            )
            packed = jnp.concatenate(
                (low.reshape(slices, 8, 512), high.reshape(slices, 8, 512)), axis=1
            )
            partials[p, :, :, pl.ds(lane, 512)] = packed.astype(BF16)
        for d in order:
            scatter_copy(p, d).start()

    def finish_patch(p):
        total = partials[p, y].astype(F32)
        for d in reversed(order):
            scatter_copy(p, d).wait_recv()
            total = total + arrived[p, d].astype(F32)
        finals[p] = (inputs[p].astype(F32) + modulation[2] * total).astype(BF16)

        @pl.when(section < sections - 1)
        def _():
            pipe_copy(p).start()

        @pl.when(section == sections - 1)
        def _():
            cfg_copy(p).start()

    def guided_copy(p, device):
        return remote(
            guided_sent.at[p], guided_out, guided_send.at[p], guided_recv, at_pipe(device)
        )

    def guide(p):
        cfg_copy(p).wait_recv()
        own, other = finals[p].astype(F32), partner[p].astype(F32)
        first = branch == 0
        own = jnp.where(first, own[:8], own[8:])
        other = jnp.where(first, other[:8], other[8:])
        conditional = jnp.where(first, own, other)
        unconditional = jnp.where(first, other, own)
        guided = unconditional + GUIDANCE_SCALE * (conditional - unconditional)
        return packed_rows(guided).astype(BF16)

    start_patch(0)

    def tick(p, carry):
        attend(p)

        @pl.when(p < patches - 1)
        def _():
            start_patch(p + 1)

        finish_patch(p)

        @pl.when(jnp.logical_and(section == sections - 1, p > 0))
        def _():
            guided_sent[p - 1] = guide(p - 1)
            guided_copy(p - 1, p - 1).start()

        return carry

    lax.fori_loop(0, patches, tick, 0)

    @pl.when(section == sections - 1)
    def _():
        guided_out[...] = guide(patches - 1)

    @pl.when(section < sections - 1)
    def _():
        guided_copy(0, sections - 1).wait_recv()

    for step in range(1, middle + 1):
        for item in (0, 1, 2):
            for way in (0, 1):
                hop(step, way, item).wait_send()
                if item != 2:
                    handed(step, way, item).wait_send()

    def drain(p, carry):
        for d in order:
            gather_copy(p, d).wait_send()
            scatter_copy(p, d).wait_send()

        @pl.when(section < sections - 1)
        def _():
            pipe_copy(p).wait_send()

        @pl.when(section == sections - 1)
        def _():
            cfg_copy(p).wait_send()

        @pl.when(jnp.logical_and(section == sections - 1, p < patches - 1))
        def _():
            guided_copy(p, p).wait_send()

        return carry

    lax.fori_loop(0, patches, drain, 0)


def local(latent, modulation, qkv_weight, out_weight, norm_gain, stale_kv):
    patches, tok_dev, model_width = latent.shape
    sections = lax.axis_size("pipe")
    slices = 8
    members = lax.axis_size("seq") // slices
    half = model_width // 2
    group_rows = slices * tok_dev
    local_width = stale_kv.shape[7]
    packed = 2 * tok_dev
    latent_packed = (
        latent.reshape(patches, tok_dev, 2, half)
        .transpose(0, 2, 1, 3)
        .reshape(patches, packed, half)
    )
    modulation_packed = jnp.broadcast_to(
        modulation[0, 0].reshape(3, 2, 1, half), (3, 2, tok_dev, half)
    ).reshape(3, packed, half)
    qkv_piece = qkv_weight[0].T
    qkv_piece = qkv_piece.reshape(2, qkv_piece.shape[0] // 2, model_width)
    out_piece = out_weight[0]
    out_piece = out_piece.reshape(2, out_piece.shape[0] // 2, model_width)
    stale = stale_kv[0, 0].reshape(2, patches, group_rows, local_width)
    dma = pltpu.SemaphoreType.DMA
    vmem = pl.BlockSpec(memory_space=pltpu.VMEM)
    blocks = members * 2
    guided, own_kv = pl.pallas_call(
        functools.partial(kernel, (sections, slices, members, patches)),
        out_shape=(
            jax.ShapeDtypeStruct((packed, half // 2), BF16),
            jax.ShapeDtypeStruct(stale.shape, BF16),
        ),
        in_specs=[vmem] * 6,
        out_specs=(vmem, vmem),
        scratch_shapes=[
            pltpu.VMEM((blocks,) + qkv_piece.shape[1:], BF16),
            pltpu.VMEM((blocks,) + out_piece.shape[1:], BF16),
            pltpu.VMEM((members - 1,) + stale.shape, BF16),
            pltpu.VMEM((patches, packed, half), BF16),
            pltpu.VMEM((patches, slices, packed, half), BF16),
            pltpu.VMEM((2, group_rows, half), BF16),
            pltpu.VMEM((patches, slices, packed, half), BF16),
            pltpu.VMEM((patches, slices, packed, half), BF16),
            pltpu.VMEM((patches, packed, half), BF16),
            pltpu.VMEM((patches, packed, half), BF16),
            pltpu.VMEM((patches, packed, half // 2), BF16),
            dma((3, 2, 4)),
            dma((3, 2, 4)),
            dma((2, 2, 4)),
            dma((2, 2, 4)),
            dma((patches, slices)),
            dma((patches, slices)),
            dma((patches, slices)),
            dma((patches, slices)),
            dma((patches,)),
            dma((patches,)),
            dma((patches,)),
            dma((patches,)),
            dma((patches,)),
            dma(()),
        ],
        compiler_params=pltpu.CompilerParams(
            collective_id=0, has_side_effects=True, vmem_limit_bytes=50 * 2**20
        ),
    )(latent_packed, modulation_packed, qkv_piece, out_piece, norm_gain[0], stale)
    guided = (
        guided.reshape(2, tok_dev, half // 2)
        .transpose(1, 0, 2)
        .reshape(1, tok_dev, half)
    )
    return guided, own_kv.reshape(stale_kv.shape)


def solution(mesh):
    placed = (
        P(None, "seq", None),
        P("pipe", "cfg", None, None),
        P("pipe", None, "seq"),
        P("pipe", "seq", None),
        P("pipe", None, None),
        P("pipe", "cfg", None, None, "seq", None, None, None),
    )
    return jax.shard_map(
        local,
        mesh=mesh,
        in_specs=placed,
        out_specs=(P("pipe", "seq", "cfg"), P("pipe", "cfg", None, None, "seq", None, None, None)),
        check_vma=False,
    )
```

```python
import functools
import math

import jax
import jax.numpy as jnp
from jax import lax
from jax.experimental import pallas as pl
from jax.experimental.pallas import tpu as pltpu
from jax.sharding import PartitionSpec as P

GUIDANCE_SCALE = 6.0
EPSILON = 1e-06
MESH = pl.DeviceIdType.MESH
F32 = jnp.float32
BF16 = jnp.bfloat16
NT = (((1,), (1,)), ((), ()))


def packed_rows(values):
    half = values.shape[-1] // 2
    return jnp.concatenate((values[..., :half], values[..., half:]), axis=-2)


def head_norm(values, gain_row):
    square = jnp.mean(values * values, axis=-1, keepdims=True)
    return values * lax.rsqrt(square + EPSILON) * gain_row


def kernel(
    sizes,
    latent,
    modulation,
    qkv_piece,
    out_piece,
    norm_gain,
    stale,
    guided_out,
    own_kv,
    qkv_all,
    out_all,
    caches,
    raw_modulation,
    gains,
    shift,
    scale,
    gate,
    inputs,
    residuals,
    features,
    mixed_left,
    queries,
    fresh,
    partials,
    arrived,
    finals,
    partner,
    guided_sent,
    local_sem,
    z_send,
    z_recv,
    pair_send,
    pair_recv,
    gather_send,
    gather_recv,
    scatter_send,
    scatter_recv,
    pipe_send,
    pipe_recv,
    cfg_send,
    cfg_recv,
    guided_send,
    guided_recv,
):
    sections, slices, members, patches = sizes
    branch = lax.axis_index("cfg")
    section = lax.axis_index("pipe")
    rank = lax.axis_index("seq")
    y = rank // members
    z = rank % members
    rows = features.shape[1] * 8
    width = features.shape[3]
    middle = members // 2
    is_first = section == 0
    is_last = section == sections - 1

    local_copies = [
        pltpu.make_async_copy(src, dst, local_sem.at[n])
        for n, (src, dst) in enumerate(
            (
                (qkv_piece, qkv_all.at[pl.ds(z * 2, 2)]),
                (stale, caches.at[0]),
                (out_piece, out_all.at[pl.ds(z * 2, 2)]),
                (modulation, raw_modulation),
                (norm_gain, gains),
                (stale, own_kv),
                (latent, inputs),
            )
        )
    ]
    for copy in local_copies[:-1]:
        copy.start()
    pl.when(is_first)(local_copies[-1].start)

    def at_z(index):
        return (branch, section, y * members + index)

    right = at_z((z + 1) % members)
    left = at_z((z + members - 1) % members)
    sibling = (1 - branch, section, rank)

    def at(plane, d):
        return (branch, plane, (y + d) % slices * members + z)

    following = (section + 1) % sections
    barrier = pltpu.get_barrier_semaphore()
    greeted = [right, left, sibling] + [at(section, d) for d in range(1, slices)]
    for d in range(slices):
        greeted += [at(following, d), at((section + sections - 1) % sections, d)]
    greeted += [at((section + d) % sections, 0) for d in range(2, sections - 1)]
    for device in greeted:
        pl.semaphore_signal(barrier, inc=1, device_id=device, device_id_type=MESH)
    pl.semaphore_wait(barrier, len(greeted))

    def remote(src, dst, send, recv, device):
        return pltpu.make_async_remote_copy(
            src_ref=src,
            dst_ref=dst,
            send_sem=send,
            recv_sem=recv,
            device_id=device,
            device_id_type=MESH,
        )

    def block(item, step, way, half, distance):
        if item in (2, 3):
            slot = distance if way == 0 else (members - distance) % members
            return caches.at[slot, item - 2]
        sign = 1 if way else members - 1
        owner = (z + sign * distance) % members
        if item == 4:
            ref = out_all.at[owner * 2 + half]
            return ref if step < middle else ref.at[:, pl.ds(way * 1024, 1024)]
        return qkv_all.at[owner * 2 + half, :, pl.ds(item * 1024, 1024)]

    def ways(item, step):
        return (0, 1) if step < middle or item == 4 else (item % 2,)

    def hop(item, step, way, lands=False):
        here = block(item, step, way, branch, step - 1)
        if item in (2, 3) or lands:
            there = block(item, step, way, branch, step)
        else:
            there = here
        send, recv = z_send.at[item, way, step - 1], z_recv.at[item, way, step - 1]
        return remote(here, there, send, recv, left if way else right)

    def handed(item, step, way, lands=False):
        ref = block(item, step, way, 1 - branch if lands else branch, step)
        send, recv = pair_send.at[item, way, step - 1], pair_recv.at[item, way, step - 1]
        return remote(ref, ref, send, recv, sibling)

    def land(item, step):
        for way in ways(item, step):
            hop(item, step, way, lands=True).wait_recv()
            if step < middle and way in ways(item, step + 1):
                hop(item, step + 1, way).start()
            if item not in (2, 3):
                handed(item, step, way).start()

    def take_handed(item):
        for step in range(1, middle + 1):
            for way in ways(item, step):
                handed(item, step, way, lands=True).wait_recv()

    items = (0, 1, 2, 3, 4)
    loaded = set()
    for item in items:
        copy = (0, 0, 1, 1, 2)[item]
        if copy not in loaded:
            local_copies[copy].wait()
            loaded.add(copy)
        for way in ways(item, 1):
            hop(item, 1, way).start()

    order = [4, 3, 5, 2, 6, 1, 7] if slices == 8 else list(range(1, slices))

    def gather_copy(p, d):
        return remote(
            features.at[p, y],
            features.at[p, y],
            gather_send.at[p, d],
            gather_recv.at[p, d],
            at(section, d),
        )

    def gather_landing(p, d):
        return remote(
            features.at[p, y],
            features.at[p, (y + slices - d) % slices],
            gather_send.at[p, d],
            gather_recv.at[p, d],
            at(section, d),
        )

    def scatter_copy(p, d, last):
        return remote(
            partials.at[p, (y + d) % slices],
            arrived.at[last, p, d],
            scatter_send.at[p, d],
            scatter_recv.at[last, p, d],
            at(section if last else following, d),
        )

    def pipe_copy(p):
        return remote(
            inputs.at[p], residuals.at[p], pipe_send.at[p], pipe_recv.at[p], at(following, 0)
        )

    def cfg_copy(p):
        return remote(finals.at[p], partner.at[p], cfg_send.at[p], cfg_recv.at[p], sibling)

    def both(left_rows):
        total = left_rows[:8] + left_rows[8:]
        return jnp.concatenate((total, total), axis=0)

    def start_patch(p):
        @pl.when(jnp.logical_not(is_first))
        def _():
            pipe_copy(p).wait_recv()
            total = residuals[p].astype(F32)
            for d in [0] + order[::-1]:
                scatter_copy(p, d, 0).wait_recv()
                total = total + arrived[0, p, d].astype(F32)
            inputs[p] = total.astype(BF16)

        x = inputs[p].astype(F32)
        count = 2 * width
        center = x - both(jnp.sum(x, axis=1, keepdims=True)) / count
        spread = both(jnp.sum(center * center, axis=1, keepdims=True)) / count
        normed = center * lax.rsqrt(spread + EPSILON)
        features[p, y] = (normed * scale[...] + shift[...]).astype(BF16)
        for d in order:
            gather_copy(p, d).start()
        pl.when(jnp.logical_not(is_last))(lambda: pipe_copy(p).start())

    def project(p):
        for d in order:
            gather_landing(p, d).wait_recv()
        stacked = features[p].astype(F32)
        mixed_left[0] = stacked[:, :8].reshape(rows, width).astype(BF16)
        mixed_left[1] = stacked[:, 8:].reshape(rows, width).astype(BF16)
        for head in range(2):
            total = None
            for piece in range(4):
                side, lane = piece // 2, (piece % 2) * 512
                weight = qkv_all[pl.ds(head * members, members), :, pl.ds(piece * 512, 512)]
                product = lax.dot_general(
                    mixed_left[side, :, pl.ds(lane, 512)],
                    weight.reshape(members * weight.shape[1], 512),
                    NT,
                    preferred_element_type=F32,
                )
                total = product if total is None else total + product
            lanes = pl.ds(head * 128, 128)
            queries[p, :, lanes] = head_norm(total[:, :128], gains[0:1]).astype(BF16)
            fresh[p, 0, :, lanes] = head_norm(total[:, 128:256], gains[1:2]).astype(BF16)
            fresh[p, 1, :, lanes] = total[:, 256:].astype(BF16)

    def attend(p):
        own_kv[0, p] = fresh[p, 0]
        own_kv[1, p] = fresh[p, 1]
        attended = []
        factor = 1.0 / math.sqrt(128)
        for head in range(2):
            lanes = pl.ds(head * 128, 128)
            query = queries[p, :, lanes]
            summed, weight_sum = None, None
            for member in range(members):
                rows_of = own_kv if member == 0 else caches.at[member]
                key_rows = rows_of[0, :, :, lanes].reshape(patches * rows, 128)
                value_rows = rows_of[1, :, :, lanes].reshape(patches * rows, 128)
                scores = lax.dot_general(query, key_rows, NT, preferred_element_type=F32)
                weights = jnp.exp(scores * factor)
                product = jnp.dot(
                    weights.astype(BF16), value_rows, preferred_element_type=F32
                )
                summed = product if summed is None else summed + product
                weight_sum = weights if weight_sum is None else weight_sum + weights
            attended.append(
                (summed / jnp.sum(weight_sum, axis=1, keepdims=True)).astype(BF16)
            )
        attended = jnp.concatenate(attended, axis=1)
        out_rows = members * 32
        for lane in range(0, width, 512):
            sides = []
            for start in (lane, width + lane):
                product = jnp.dot(
                    attended,
                    out_all[:, :, pl.ds(start, 512)].reshape(out_rows, 512),
                    preferred_element_type=F32,
                )
                sides.append(product.reshape(slices, 8, 512) * gate[:, pl.ds(start, 512)])
            packed = jnp.concatenate(sides, axis=1)
            partials[p, :, :, pl.ds(lane, 512)] = packed.astype(BF16)

        @pl.when(is_last)
        def _():
            for d in order:
                scatter_copy(p, d, 1).start()

        @pl.when(jnp.logical_not(is_last))
        def _():
            for d in order + [0]:
                scatter_copy(p, d, 0).start()

    def finish_patch(p):
        total = inputs[p].astype(F32) + partials[p, y].astype(F32)
        for d in reversed(order):
            scatter_copy(p, d, 1).wait_recv()
            total = total + arrived[1, p, d].astype(F32)
        finals[p] = total.astype(BF16)
        cfg_copy(p).start()

    def guided_copy(p, device):
        return remote(
            guided_sent.at[p], guided_out, guided_send.at[p], guided_recv, at(device, 0)
        )

    def guide(p):
        cfg_copy(p).wait_recv()
        own, other = finals[p].astype(F32), partner[p].astype(F32)
        first = branch == 0
        own = jnp.where(first, own[:8], own[8:])
        other = jnp.where(first, other[:8], other[8:])
        conditional = jnp.where(first, own, other)
        unconditional = jnp.where(first, other, own)
        guided = unconditional + GUIDANCE_SCALE * (conditional - unconditional)
        return packed_rows(guided).astype(BF16)

    def send_guided(p):
        guided_sent[p] = guide(p)
        guided_copy(p, p).start()

    local_copies[3].wait()
    for lane in range(16):
        lanes = pl.ds(lane % 8 * 128, 128)
        half = pl.ds(lane // 8 * 8, 8)
        row = lambda kind: jnp.broadcast_to(raw_modulation[pl.ds(kind * 16 + lane, 1), :], (8, 128))
        shift[half, lanes] = row(0)
        scale[half, lanes] = 1.0 + row(1)
        gate[:, pl.ds(lane * 128, 128)] = row(2)

    def each_patch(body):
        def step(p, carry):
            body(p)
            return carry

        lax.fori_loop(0, patches, step, 0)

    @pl.when(is_first)
    def _():
        local_copies[-1].wait()
        each_patch(start_patch)

    for step in range(1, middle + 1):
        for item in items:
            if step == middle and item in (2, 3):
                continue
            land(item, step)
    take_handed(0)
    take_handed(1)
    local_copies[4].wait()
    pl.when(is_first)(lambda: each_patch(project))
    for item in (2, 3):
        land(item, middle)
    take_handed(4)
    local_copies[5].wait()

    def tick(p):
        @pl.when(jnp.logical_not(is_first))
        def _():
            pl.when(p < patches - 1)(lambda: start_patch(p + 1))
            project(p)

        attend(p)

        @pl.when(jnp.logical_and(is_last, p > 0))
        def _():
            finish_patch(p - 1)

        @pl.when(jnp.logical_and(is_last, p > 1))
        def _():
            send_guided(p - 2)

    pl.when(jnp.logical_not(is_first))(lambda: start_patch(0))
    each_patch(tick)

    @pl.when(is_last)
    def _():
        finish_patch(patches - 1)
        send_guided(patches - 2)
        guided_out[...] = guide(patches - 1)

    @pl.when(jnp.logical_not(is_last))
    def _():
        guided_copy(0, sections - 1).wait_recv()

    for step in range(1, middle + 1):
        for item in items:
            for way in ways(item, step):
                hop(item, step, way).wait_send()
                if item not in (2, 3):
                    handed(item, step, way).wait_send()

    def drain(p):
        for d in order:
            gather_copy(p, d).wait_send()

        @pl.when(jnp.logical_not(is_last))
        def _():
            pipe_copy(p).wait_send()
            for d in order + [0]:
                scatter_copy(p, d, 0).wait_send()

        @pl.when(is_last)
        def _():
            cfg_copy(p).wait_send()
            for d in order:
                scatter_copy(p, d, 1).wait_send()

        @pl.when(jnp.logical_and(is_last, p < patches - 1))
        def _():
            guided_copy(p, p).wait_send()

    each_patch(drain)


def local(latent, modulation, qkv_weight, out_weight, norm_gain, stale_kv):
    patches, tok_dev, model_width = latent.shape
    sections = lax.axis_size("pipe")
    slices = 8
    members = lax.axis_size("seq") // slices
    half = model_width // 2
    group_rows = slices * tok_dev
    local_width = stale_kv.shape[7]
    packed = 2 * tok_dev
    latent_packed = (
        latent.reshape(patches, tok_dev, 2, half)
        .transpose(0, 2, 1, 3)
        .reshape(patches, packed, half)
    )
    modulation_rows = modulation.reshape(3 * model_width // 128, 128)
    qkv_piece = qkv_weight[0].T
    qkv_piece = qkv_piece.reshape(2, qkv_piece.shape[0] // 2, model_width)
    out_piece = out_weight[0]
    out_piece = out_piece.reshape(2, out_piece.shape[0] // 2, model_width)
    stale = stale_kv[0, 0].reshape(2, patches, group_rows, local_width)
    dma = pltpu.SemaphoreType.DMA
    vmem = pl.BlockSpec(memory_space=pltpu.VMEM)
    blocks = members * 2
    guided, own_kv = pl.pallas_call(
        functools.partial(kernel, (sections, slices, members, patches)),
        out_shape=(
            jax.ShapeDtypeStruct((packed, half // 2), BF16),
            jax.ShapeDtypeStruct(stale.shape, BF16),
        ),
        in_specs=[pl.BlockSpec(memory_space=pltpu.HBM)] * 6,
        out_specs=(vmem, vmem),
        scratch_shapes=[
            pltpu.VMEM((blocks,) + qkv_piece.shape[1:], BF16),
            pltpu.VMEM((blocks,) + out_piece.shape[1:], BF16),
            pltpu.VMEM((members,) + stale.shape, BF16),
            pltpu.VMEM(modulation_rows.shape, F32),
            pltpu.VMEM(norm_gain.shape[1:], F32),
            pltpu.VMEM((packed, half), F32),
            pltpu.VMEM((packed, half), F32),
            pltpu.VMEM((tok_dev, model_width), F32),
            pltpu.VMEM((patches, packed, half), BF16),
            pltpu.VMEM((patches, packed, half), BF16),
            pltpu.VMEM((patches, slices, packed, half), BF16),
            pltpu.VMEM((2, group_rows, half), BF16),
            pltpu.VMEM((patches, group_rows, local_width), BF16),
            pltpu.VMEM((patches, 2, group_rows, local_width), BF16),
            pltpu.VMEM((patches, slices, packed, half), BF16),
            pltpu.VMEM((2, patches, slices, packed, half), BF16),
            pltpu.VMEM((patches, packed, half), BF16),
            pltpu.VMEM((patches, packed, half), BF16),
            pltpu.VMEM((patches, packed, half // 2), BF16),
            dma((7,)),
            dma((5, 2, 4)),
            dma((5, 2, 4)),
            dma((5, 2, 4)),
            dma((5, 2, 4)),
            dma((patches, slices)),
            dma((patches, slices)),
            dma((patches, slices)),
            dma((2, patches, slices)),
            dma((patches,)),
            dma((patches,)),
            dma((patches,)),
            dma((patches,)),
            dma((patches,)),
            dma(()),
        ],
        compiler_params=pltpu.CompilerParams(
            collective_id=0, has_side_effects=True, vmem_limit_bytes=63 * 2**20 + 2**19
        ),
    )(latent_packed, modulation_rows, qkv_piece, out_piece, norm_gain[0], stale)
    guided = (
        guided.reshape(2, tok_dev, half // 2)
        .transpose(1, 0, 2)
        .reshape(1, tok_dev, half)
    )
    return guided, own_kv.reshape(stale_kv.shape)


def solution(mesh):
    placed = (
        P(None, "seq", None),
        P("pipe", "cfg", None, None),
        P("pipe", None, "seq"),
        P("pipe", "seq", None),
        P("pipe", None, None),
        P("pipe", "cfg", None, None, "seq", None, None, None),
    )
    return jax.shard_map(
        local,
        mesh=mesh,
        in_specs=placed,
        out_specs=(P("pipe", "seq", "cfg"), P("pipe", "cfg", None, None, "seq", None, None, None)),
        check_vma=False,
    )
```

```python
import functools
import math

import jax
import jax.numpy as jnp
from jax import lax
from jax.experimental import pallas as pl
from jax.experimental.pallas import tpu as pltpu
from jax.sharding import PartitionSpec as P

GUIDANCE_SCALE = 6.0
EPSILON = 1e-06
MESH = pl.DeviceIdType.MESH
F32 = jnp.float32
BF16 = jnp.bfloat16
NT = (((1,), (1,)), ((), ()))


def packed_rows(values):
    half = values.shape[-1] // 2
    return jnp.concatenate((values[..., :half], values[..., half:]), axis=-2)


def head_norm(values, gain_row):
    square = jnp.mean(values * values, axis=-1, keepdims=True)
    return values * lax.rsqrt(square + EPSILON) * gain_row


def kernel(
    sizes,
    latent,
    modulation,
    qkv_piece,
    out_piece,
    norm_gain,
    stale,
    guided_out,
    own_kv,
    qkv_all,
    out_all,
    caches,
    helped,
    raw_modulation,
    gains,
    shift,
    scale,
    gate,
    inputs,
    residuals,
    features,
    mixed_left,
    queries,
    fresh,
    partials,
    arrived,
    finals,
    partner,
    guided_sent,
    local_sem,
    z_send,
    z_recv,
    pair_send,
    pair_recv,
    help_send,
    help_recv,
    gather_send,
    gather_recv,
    scatter_send,
    scatter_recv,
    pipe_send,
    pipe_recv,
    cfg_send,
    cfg_recv,
    guided_send,
    guided_recv,
):
    sections, slices, members, patches = sizes
    branch = lax.axis_index("cfg")
    section = lax.axis_index("pipe")
    rank = lax.axis_index("seq")
    y = rank // members
    z = rank % members
    rows = features.shape[1] * 8
    width = features.shape[3]
    middle = members // 2
    is_first = section == 0
    is_last = section == sections - 1

    local_copies = [
        pltpu.make_async_copy(src, dst, local_sem.at[n])
        for n, (src, dst) in enumerate(
            (
                (qkv_piece, qkv_all.at[pl.ds(z * 2, 2)]),
                (stale, caches.at[0]),
                (out_piece, out_all.at[pl.ds(z * 2, 2)]),
                (modulation, raw_modulation),
                (norm_gain, gains),
                (stale, own_kv),
                (latent, inputs),
            )
        )
    ]
    for copy in local_copies[:-1]:
        copy.start()
    pl.when(is_first)(local_copies[-1].start)

    def at_z(index):
        return (branch, section, y * members + index)

    right = at_z((z + 1) % members)
    left = at_z((z + members - 1) % members)
    sibling = (1 - branch, section, rank)

    def at(plane, d):
        return (branch, plane, (y + d) % slices * members + z)

    following = (section + 1) % sections
    barrier = pltpu.get_barrier_semaphore()
    greeted = [right, left, sibling] + [at(section, d) for d in range(1, slices)]
    for d in range(slices):
        greeted += [at(following, d), at((section + sections - 1) % sections, d)]
    greeted += [at((section + d) % sections, 0) for d in range(2, sections - 1)]
    for device in greeted:
        pl.semaphore_signal(barrier, inc=1, device_id=device, device_id_type=MESH)
    pl.semaphore_wait(barrier, len(greeted))

    def remote(src, dst, send, recv, device):
        return pltpu.make_async_remote_copy(
            src_ref=src,
            dst_ref=dst,
            send_sem=send,
            recv_sem=recv,
            device_id=device,
            device_id_type=MESH,
        )

    def block(item, step, way, half, distance):
        if item in (2, 3, 5):
            slot = distance if way == 0 else (members - distance) % members
            return helped.at[slot] if item == 5 else caches.at[slot, item - 2]
        sign = 1 if way else members - 1
        owner = (z + sign * distance) % members
        if item == 4:
            ref = out_all.at[owner * 2 + half]
            return ref if step < middle else ref.at[:, pl.ds(way * 1024, 1024)]
        return qkv_all.at[owner * 2 + half, :, pl.ds(item * 1024, 1024)]

    def ways(item, step):
        return (0, 1) if step < middle or item == 4 else (item % 2,)

    def hop(item, step, way, lands=False):
        here = block(item, step, way, branch, step - 1)
        if item in (2, 3, 5) or lands:
            there = block(item, step, way, branch, step)
        else:
            there = here
        send, recv = z_send.at[item, way, step - 1], z_recv.at[item, way, step - 1]
        return remote(here, there, send, recv, left if way else right)

    def handed(item, step, way, lands=False):
        ref = block(item, step, way, 1 - branch if lands else branch, step)
        send, recv = pair_send.at[item, way, step - 1], pair_recv.at[item, way, step - 1]
        return remote(ref, ref, send, recv, sibling)

    def help_out():
        return remote(
            caches.at[0, 1], helped.at[0], help_send.at[0], help_recv.at[0], at(sections - 1, 0)
        )

    def help_back(slot):
        return remote(
            helped.at[slot], caches.at[slot, 1], help_send.at[slot], help_recv.at[slot], at(0, 0)
        )

    def land(item, step):
        for way in ways(item, step):
            hop(item, step, way, lands=True).wait_recv()
            if step < middle and way in ways(item, step + 1):
                hop(item, step + 1, way).start()
            if item == 5:
                help_back(step if way == 0 else members - step).start()
            elif item not in (2, 3):
                handed(item, step, way).start()

    def take_handed(item):
        for step in range(1, middle + 1):
            for way in ways(item, step):
                handed(item, step, way, lands=True).wait_recv()

    items = (0, 1, 2, 3, 4)
    def here(item):
        return jnp.logical_not(is_first) if item == 3 else section >= 0

    for n in range(3):
        local_copies[n].wait()
    pl.when(is_first)(lambda: help_out().start())

    @pl.when(is_last)
    def _():
        help_out().wait_recv()
        for way in ways(5, 1):
            hop(5, 1, way).start()
        for step in range(1, middle + 1):
            land(5, step)

    for item in items:
        @pl.when(here(item))
        def _():
            for way in ways(item, 1):
                hop(item, 1, way).start()

    order = [4, 3, 5, 2, 6, 1, 7] if slices == 8 else list(range(1, slices))

    def gather_copy(p, d):
        return remote(
            features.at[p, y],
            features.at[p, y],
            gather_send.at[p, d],
            gather_recv.at[p, d],
            at(section, d),
        )

    def gather_landing(p, d):
        return remote(
            features.at[p, y],
            features.at[p, (y + slices - d) % slices],
            gather_send.at[p, d],
            gather_recv.at[p, d],
            at(section, d),
        )

    def scatter_copy(p, d, last):
        return remote(
            partials.at[p, (y + d) % slices],
            arrived.at[last, p, d],
            scatter_send.at[p, d],
            scatter_recv.at[last, p, d],
            at(section if last else following, d),
        )

    def pipe_copy(p):
        return remote(
            inputs.at[p], residuals.at[p], pipe_send.at[p], pipe_recv.at[p], at(following, 0)
        )

    def cfg_copy(p):
        return remote(finals.at[p], partner.at[p], cfg_send.at[p], cfg_recv.at[p], sibling)

    def both(left_rows):
        total = left_rows[:8] + left_rows[8:]
        return jnp.concatenate((total, total), axis=0)

    def start_patch(p):
        @pl.when(jnp.logical_not(is_first))
        def _():
            pipe_copy(p).wait_recv()
            total = residuals[p].astype(F32)
            for d in [0] + order[::-1]:
                scatter_copy(p, d, 0).wait_recv()
                total = total + arrived[0, p, d].astype(F32)
            inputs[p] = total.astype(BF16)

        x = inputs[p].astype(F32)
        count = 2 * width
        center = x - both(jnp.sum(x, axis=1, keepdims=True)) / count
        spread = both(jnp.sum(center * center, axis=1, keepdims=True)) / count
        normed = center * lax.rsqrt(spread + EPSILON)
        features[p, y] = (normed * scale[...] + shift[...]).astype(BF16)
        for d in order:
            gather_copy(p, d).start()
        pl.when(jnp.logical_not(is_last))(lambda: pipe_copy(p).start())

    def project(p):
        for d in order:
            gather_landing(p, d).wait_recv()
        stacked = features[p].astype(F32)
        mixed_left[0] = stacked[:, :8].reshape(rows, width).astype(BF16)
        mixed_left[1] = stacked[:, 8:].reshape(rows, width).astype(BF16)
        for head in range(2):
            total = None
            for piece in range(4):
                side, lane = piece // 2, (piece % 2) * 512
                weight = qkv_all[pl.ds(head * members, members), :, pl.ds(piece * 512, 512)]
                product = lax.dot_general(
                    mixed_left[side, :, pl.ds(lane, 512)],
                    weight.reshape(members * weight.shape[1], 512),
                    NT,
                    preferred_element_type=F32,
                )
                total = product if total is None else total + product
            lanes = pl.ds(head * 128, 128)
            queries[p, :, lanes] = head_norm(total[:, :128], gains[0:1]).astype(BF16)
            fresh[p, 0, :, lanes] = head_norm(total[:, 128:256], gains[1:2]).astype(BF16)
            fresh[p, 1, :, lanes] = total[:, 256:].astype(BF16)

    def attend(p):
        own_kv[0, p] = fresh[p, 0]
        own_kv[1, p] = fresh[p, 1]
        attended = []
        factor = 1.0 / math.sqrt(128)
        for head in range(2):
            lanes = pl.ds(head * 128, 128)
            query = queries[p, :, lanes]
            summed, weight_sum = None, None
            for member in range(members):
                rows_of = own_kv if member == 0 else caches.at[member]
                key_rows = rows_of[0, :, :, lanes].reshape(patches * rows, 128)
                value_rows = rows_of[1, :, :, lanes].reshape(patches * rows, 128)
                scores = lax.dot_general(query, key_rows, NT, preferred_element_type=F32)
                weights = jnp.exp(scores * factor)
                product = jnp.dot(
                    weights.astype(BF16), value_rows, preferred_element_type=F32
                )
                summed = product if summed is None else summed + product
                weight_sum = weights if weight_sum is None else weight_sum + weights
            attended.append(
                (summed / jnp.sum(weight_sum, axis=1, keepdims=True)).astype(BF16)
            )
        attended = jnp.concatenate(attended, axis=1)
        out_rows = members * 32
        for lane in range(0, width, 512):
            sides = []
            for start in (lane, width + lane):
                product = jnp.dot(
                    attended,
                    out_all[:, :, pl.ds(start, 512)].reshape(out_rows, 512),
                    preferred_element_type=F32,
                )
                sides.append(product.reshape(slices, 8, 512) * gate[:, pl.ds(start, 512)])
            packed = jnp.concatenate(sides, axis=1)
            partials[p, :, :, pl.ds(lane, 512)] = packed.astype(BF16)

        @pl.when(is_last)
        def _():
            for d in order:
                scatter_copy(p, d, 1).start()

        @pl.when(jnp.logical_not(is_last))
        def _():
            for d in order + [0]:
                scatter_copy(p, d, 0).start()

    def finish_patch(p):
        total = inputs[p].astype(F32) + partials[p, y].astype(F32)
        for d in reversed(order):
            scatter_copy(p, d, 1).wait_recv()
            total = total + arrived[1, p, d].astype(F32)
        finals[p] = total.astype(BF16)
        cfg_copy(p).start()

    def guided_copy(p, device):
        return remote(
            guided_sent.at[p], guided_out, guided_send.at[p], guided_recv, at(device, 0)
        )

    def guide(p):
        cfg_copy(p).wait_recv()
        own, other = finals[p].astype(F32), partner[p].astype(F32)
        first = branch == 0
        own = jnp.where(first, own[:8], own[8:])
        other = jnp.where(first, other[:8], other[8:])
        conditional = jnp.where(first, own, other)
        unconditional = jnp.where(first, other, own)
        guided = unconditional + GUIDANCE_SCALE * (conditional - unconditional)
        return packed_rows(guided).astype(BF16)

    def send_guided(p):
        guided_sent[p] = guide(p)
        guided_copy(p, p).start()

    local_copies[3].wait()
    for lane in range(16):
        lanes = pl.ds(lane % 8 * 128, 128)
        half = pl.ds(lane // 8 * 8, 8)
        row = lambda kind: jnp.broadcast_to(raw_modulation[pl.ds(kind * 16 + lane, 1), :], (8, 128))
        shift[half, lanes] = row(0)
        scale[half, lanes] = 1.0 + row(1)
        gate[:, pl.ds(lane * 128, 128)] = row(2)

    def each_patch(body):
        def step(p, carry):
            body(p)
            return carry

        lax.fori_loop(0, patches, step, 0)

    @pl.when(is_first)
    def _():
        local_copies[-1].wait()
        each_patch(start_patch)

    for step in range(1, middle + 1):
        for item in items:
            if step == middle and item in (2, 3):
                continue
            pl.when(here(item))(functools.partial(land, item, step))
    take_handed(0)
    take_handed(1)
    local_copies[4].wait()
    pl.when(is_first)(lambda: each_patch(project))
    land(2, middle)
    pl.when(here(3))(functools.partial(land, 3, middle))

    @pl.when(is_first)
    def _():
        for slot in range(1, members):
            help_back(slot).wait_recv()

    take_handed(4)
    local_copies[5].wait()

    def tick(p):
        @pl.when(jnp.logical_not(is_first))
        def _():
            project(p)
            pl.when(p < patches - 1)(lambda: start_patch(p + 1))

        attend(p)

        @pl.when(jnp.logical_and(is_last, p > 0))
        def _():
            finish_patch(p - 1)

        @pl.when(jnp.logical_and(is_last, p > 1))
        def _():
            send_guided(p - 2)

    pl.when(jnp.logical_not(is_first))(lambda: start_patch(0))
    each_patch(tick)

    @pl.when(is_last)
    def _():
        finish_patch(patches - 1)
        send_guided(patches - 2)
        guided_out[...] = guide(patches - 1)

    @pl.when(jnp.logical_not(is_last))
    def _():
        guided_copy(0, sections - 1).wait_recv()

    def drain_ring(item):
        for step in range(1, middle + 1):
            for way in ways(item, step):
                hop(item, step, way).wait_send()
                if item not in (2, 3, 5):
                    handed(item, step, way).wait_send()

    for item in items:
        pl.when(here(item))(functools.partial(drain_ring, item))
    pl.when(is_first)(lambda: help_out().wait_send())

    @pl.when(is_last)
    def _():
        drain_ring(5)
        for slot in range(1, members):
            help_back(slot).wait_send()

    def drain(p):
        for d in order:
            gather_copy(p, d).wait_send()

        @pl.when(jnp.logical_not(is_last))
        def _():
            pipe_copy(p).wait_send()
            for d in order + [0]:
                scatter_copy(p, d, 0).wait_send()

        @pl.when(is_last)
        def _():
            cfg_copy(p).wait_send()
            for d in order:
                scatter_copy(p, d, 1).wait_send()

        @pl.when(jnp.logical_and(is_last, p < patches - 1))
        def _():
            guided_copy(p, p).wait_send()

    each_patch(drain)


def local(latent, modulation, qkv_weight, out_weight, norm_gain, stale_kv):
    patches, tok_dev, model_width = latent.shape
    sections = lax.axis_size("pipe")
    slices = 8
    members = lax.axis_size("seq") // slices
    half = model_width // 2
    group_rows = slices * tok_dev
    local_width = stale_kv.shape[7]
    packed = 2 * tok_dev
    latent_packed = (
        latent.reshape(patches, tok_dev, 2, half)
        .transpose(0, 2, 1, 3)
        .reshape(patches, packed, half)
    )
    modulation_rows = modulation.reshape(3 * model_width // 128, 128)
    qkv_piece = qkv_weight[0].T
    qkv_piece = qkv_piece.reshape(2, qkv_piece.shape[0] // 2, model_width)
    out_piece = out_weight[0]
    out_piece = out_piece.reshape(2, out_piece.shape[0] // 2, model_width)
    stale = stale_kv[0, 0].reshape(2, patches, group_rows, local_width)
    dma = pltpu.SemaphoreType.DMA
    vmem = pl.BlockSpec(memory_space=pltpu.VMEM)
    blocks = members * 2
    guided, own_kv = pl.pallas_call(
        functools.partial(kernel, (sections, slices, members, patches)),
        out_shape=(
            jax.ShapeDtypeStruct((packed, half // 2), BF16),
            jax.ShapeDtypeStruct(stale.shape, BF16),
        ),
        in_specs=[pl.BlockSpec(memory_space=pltpu.HBM)] * 6,
        out_specs=(vmem, vmem),
        scratch_shapes=[
            pltpu.VMEM((blocks,) + qkv_piece.shape[1:], BF16),
            pltpu.VMEM((blocks,) + out_piece.shape[1:], BF16),
            pltpu.VMEM((members,) + stale.shape, BF16),
            pltpu.VMEM((members,) + stale.shape[1:], BF16),
            pltpu.VMEM(modulation_rows.shape, F32),
            pltpu.VMEM(norm_gain.shape[1:], F32),
            pltpu.VMEM((packed, half), F32),
            pltpu.VMEM((packed, half), F32),
            pltpu.VMEM((tok_dev, model_width), F32),
            pltpu.VMEM((patches, packed, half), BF16),
            pltpu.VMEM((patches, packed, half), BF16),
            pltpu.VMEM((patches, slices, packed, half), BF16),
            pltpu.VMEM((2, group_rows, half), BF16),
            pltpu.VMEM((patches, group_rows, local_width), BF16),
            pltpu.VMEM((patches, 2, group_rows, local_width), BF16),
            pltpu.VMEM((patches, slices, packed, half), BF16),
            pltpu.VMEM((2, patches, slices, packed, half), BF16),
            pltpu.VMEM((patches, packed, half), BF16),
            pltpu.VMEM((patches, packed, half), BF16),
            pltpu.VMEM((patches, packed, half // 2), BF16),
            dma((7,)),
            dma((6, 2, 4)),
            dma((6, 2, 4)),
            dma((6, 2, 4)),
            dma((6, 2, 4)),
            dma((members,)),
            dma((members,)),
            dma((patches, slices)),
            dma((patches, slices)),
            dma((patches, slices)),
            dma((2, patches, slices)),
            dma((patches,)),
            dma((patches,)),
            dma((patches,)),
            dma((patches,)),
            dma((patches,)),
            dma(()),
        ],
        compiler_params=pltpu.CompilerParams(
            collective_id=0, has_side_effects=True, vmem_limit_bytes=63 * 2**20 + 2**19
        ),
    )(latent_packed, modulation_rows, qkv_piece, out_piece, norm_gain[0], stale)
    guided = (
        guided.reshape(2, tok_dev, half // 2)
        .transpose(1, 0, 2)
        .reshape(1, tok_dev, half)
    )
    return guided, own_kv.reshape(stale_kv.shape)


def solution(mesh):
    placed = (
        P(None, "seq", None),
        P("pipe", "cfg", None, None),
        P("pipe", None, "seq"),
        P("pipe", "seq", None),
        P("pipe", None, None),
        P("pipe", "cfg", None, None, "seq", None, None, None),
    )
    return jax.shard_map(
        local,
        mesh=mesh,
        in_specs=placed,
        out_specs=(P("pipe", "seq", "cfg"), P("pipe", "cfg", None, None, "seq", None, None, None)),
        check_vma=False,
    )
```

```python
import functools
import math

import jax
import jax.numpy as jnp
from jax import lax
from jax.experimental import pallas as pl
from jax.experimental.pallas import tpu as pltpu
from jax.sharding import PartitionSpec as P

GUIDANCE_SCALE = 6.0
EPSILON = 1e-06
MESH = pl.DeviceIdType.MESH
F32 = jnp.float32
BF16 = jnp.bfloat16
NT = (((1,), (1,)), ((), ()))


def packed_rows(values):
    half = values.shape[-1] // 2
    return jnp.concatenate((values[..., :half], values[..., half:]), axis=-2)


def head_norm(values, gain_row):
    square = jnp.mean(values * values, axis=-1, keepdims=True)
    return values * lax.rsqrt(square + EPSILON) * gain_row


def kernel(
    sizes,
    latent,
    modulation,
    qkv_piece,
    out_piece,
    norm_gain,
    stale,
    guided_out,
    own_kv,
    qkv_all,
    out_all,
    caches,
    helped,
    raw_modulation,
    gains,
    shift,
    scale,
    gate,
    inputs,
    residuals,
    features,
    mixed_left,
    queries,
    fresh,
    partials,
    arrived,
    finals,
    partner,
    guided_sent,
    local_sem,
    z_send,
    z_recv,
    pair_send,
    pair_recv,
    help_send,
    help_recv,
    gather_send,
    gather_recv,
    scatter_send,
    scatter_recv,
    pipe_send,
    pipe_recv,
    cfg_send,
    cfg_recv,
    guided_send,
    guided_recv,
):
    sections, slices, members, patches = sizes
    branch = lax.axis_index("cfg")
    section = lax.axis_index("pipe")
    rank = lax.axis_index("seq")
    y = rank // members
    z = rank % members
    rows = features.shape[1] * 8
    width = features.shape[3]
    middle = members // 2
    is_first = section == 0
    is_last = section == sections - 1

    local_copies = [
        pltpu.make_async_copy(src, dst, local_sem.at[n])
        for n, (src, dst) in enumerate(
            (
                (qkv_piece, qkv_all.at[pl.ds(z * 2, 2)]),
                (stale, caches.at[0]),
                (out_piece, out_all.at[pl.ds(z * 2, 2)]),
                (modulation, raw_modulation),
                (norm_gain, gains),
                (stale, own_kv),
                (latent, inputs),
            )
        )
    ]
    for copy in local_copies[:-1]:
        copy.start()
    pl.when(is_first)(local_copies[-1].start)

    def at_z(index):
        return (branch, section, y * members + index)

    right = at_z((z + 1) % members)
    left = at_z((z + members - 1) % members)
    sibling = (1 - branch, section, rank)

    def at(plane, d):
        return (branch, plane, (y + d) % slices * members + z)

    following = (section + 1) % sections
    barrier = pltpu.get_barrier_semaphore()
    greeted = [right, left, sibling] + [at(section, d) for d in range(1, slices)]
    for d in range(slices):
        greeted += [at(following, d), at((section + sections - 1) % sections, d)]
    greeted += [at((section + d) % sections, 0) for d in range(2, sections - 1)]
    for device in greeted:
        pl.semaphore_signal(barrier, inc=1, device_id=device, device_id_type=MESH)
    pl.semaphore_wait(barrier, len(greeted))

    def remote(src, dst, send, recv, device):
        return pltpu.make_async_remote_copy(
            src_ref=src,
            dst_ref=dst,
            send_sem=send,
            recv_sem=recv,
            device_id=device,
            device_id_type=MESH,
        )

    def block(item, step, way, half, distance):
        if item in (2, 3, 5):
            slot = distance if way == 0 else (members - distance) % members
            return helped.at[slot] if item == 5 else caches.at[slot, item - 2]
        sign = 1 if way else members - 1
        owner = (z + sign * distance) % members
        if item == 4:
            ref = out_all.at[owner * 2 + half]
            return ref if step < middle else ref.at[:, pl.ds(way * 1024, 1024)]
        return qkv_all.at[owner * 2 + half, :, pl.ds(item * 1024, 1024)]

    def ways(item, step):
        return (0, 1) if step < middle or item == 4 else (item % 2,)

    def hop(item, step, way, lands=False):
        here = block(item, step, way, branch, step - 1)
        if item in (2, 3, 5) or lands:
            there = block(item, step, way, branch, step)
        else:
            there = here
        send, recv = z_send.at[item, way, step - 1], z_recv.at[item, way, step - 1]
        return remote(here, there, send, recv, left if way else right)

    def handed(item, step, way, lands=False):
        ref = block(item, step, way, 1 - branch if lands else branch, step)
        send, recv = pair_send.at[item, way, step - 1], pair_recv.at[item, way, step - 1]
        return remote(ref, ref, send, recv, sibling)

    def help_out():
        return remote(
            caches.at[0, 1], helped.at[0], help_send.at[0], help_recv.at[0], at(sections - 1, 0)
        )

    def help_back(slot):
        return remote(
            helped.at[slot], caches.at[slot, 1], help_send.at[slot], help_recv.at[slot], at(0, 0)
        )

    def land(item, step):
        for way in ways(item, step):
            hop(item, step, way, lands=True).wait_recv()
            if step < middle and way in ways(item, step + 1):
                hop(item, step + 1, way).start()
            if item == 5:
                help_back(step if way == 0 else members - step).start()
            elif item not in (2, 3):
                handed(item, step, way).start()

    def take_handed(item):
        for step in range(1, middle + 1):
            for way in ways(item, step):
                handed(item, step, way, lands=True).wait_recv()

    items = (0, 1, 2, 3, 4)
    def here(item):
        return jnp.logical_not(is_first) if item == 3 else section >= 0

    for n in range(3):
        local_copies[n].wait()
    pl.when(is_first)(lambda: help_out().start())

    @pl.when(is_last)
    def _():
        help_out().wait_recv()
        for way in ways(5, 1):
            hop(5, 1, way).start()
        for step in range(1, middle + 1):
            land(5, step)

    for item in items:
        @pl.when(here(item))
        def _():
            for way in ways(item, 1):
                hop(item, 1, way).start()

    order = [4, 3, 5, 2, 6, 1, 7] if slices == 8 else list(range(1, slices))

    def gather_copy(p, d):
        return remote(
            features.at[p, y],
            features.at[p, y],
            gather_send.at[p, d],
            gather_recv.at[p, d],
            at(section, d),
        )

    def gather_landing(p, d):
        return remote(
            features.at[p, y],
            features.at[p, (y + slices - d) % slices],
            gather_send.at[p, d],
            gather_recv.at[p, d],
            at(section, d),
        )

    def scatter_copy(p, d, last):
        return remote(
            partials.at[p, (y + d) % slices],
            arrived.at[last, p, d],
            scatter_send.at[p, d],
            scatter_recv.at[last, p, d],
            at(section if last else following, d),
        )

    def pipe_copy(p):
        return remote(
            inputs.at[p], residuals.at[p], pipe_send.at[p], pipe_recv.at[p], at(following, 0)
        )

    def cfg_copy(p):
        return remote(finals.at[p], partner.at[p], cfg_send.at[p], cfg_recv.at[p], sibling)

    def both(left_rows):
        total = left_rows[:8] + left_rows[8:]
        return jnp.concatenate((total, total), axis=0)

    def start_patch(p):
        @pl.when(jnp.logical_not(is_first))
        def _():
            pipe_copy(p).wait_recv()
            total = residuals[p].astype(F32)
            for d in [0] + order[::-1]:
                scatter_copy(p, d, 0).wait_recv()
                total = total + arrived[0, p, d].astype(F32)
            inputs[p] = total.astype(BF16)

        x = inputs[p].astype(F32)
        count = 2 * width
        center = x - both(jnp.sum(x, axis=1, keepdims=True)) / count
        spread = both(jnp.sum(center * center, axis=1, keepdims=True)) / count
        normed = center * lax.rsqrt(spread + EPSILON)
        features[p, y] = (normed * scale[...] + shift[...]).astype(BF16)
        for d in order:
            gather_copy(p, d).start()
        pl.when(jnp.logical_not(is_last))(lambda: pipe_copy(p).start())

    def project(p):
        for d in order:
            gather_landing(p, d).wait_recv()
        stacked = features[p].astype(F32)
        mixed_left[0] = stacked[:, :8].reshape(rows, width).astype(BF16)
        mixed_left[1] = stacked[:, 8:].reshape(rows, width).astype(BF16)
        for head in range(2):
            total = None
            for piece in range(4):
                side, lane = piece // 2, (piece % 2) * 512
                weight = qkv_all[pl.ds(head * members, members), :, pl.ds(piece * 512, 512)]
                product = lax.dot_general(
                    mixed_left[side, :, pl.ds(lane, 512)],
                    weight.reshape(members * weight.shape[1], 512),
                    NT,
                    preferred_element_type=F32,
                )
                total = product if total is None else total + product
            lanes = pl.ds(head * 128, 128)
            queries[p, pl.ds(head * rows, rows), lanes] = head_norm(total[:, :128], gains[0:1]).astype(BF16)
            fresh[p, 0, :, lanes] = head_norm(total[:, 128:256], gains[1:2]).astype(BF16)
            fresh[p, 1, :, lanes] = total[:, 256:].astype(BF16)

    def attend(p):
        own_kv[0, p] = fresh[p, 0]
        own_kv[1, p] = fresh[p, 1]
        factor = math.log2(math.e) / math.sqrt(128)
        query = queries[p]
        summed, weight_sum = None, None
        for first in range(0, members, 4):
            blocks = [own_kv if n == 0 else caches.at[n] for n in range(first, first + 4)]
            scores = [
                lax.dot_general(
                    query,
                    block[0].reshape(patches * rows, 256),
                    NT,
                    preferred_element_type=F32,
                )
                for block in blocks
            ]
            for block, score in zip(blocks, scores):
                weights = jnp.exp2(score * factor)
                product = jnp.dot(
                    weights.astype(BF16),
                    block[1].reshape(patches * rows, 256),
                    preferred_element_type=F32,
                )
                summed = product if summed is None else summed + product
                weight_sum = weights if weight_sum is None else weight_sum + weights
        weight_sum = jnp.sum(weight_sum, axis=1, keepdims=True)
        attended = [
            (summed[:rows, :128] / weight_sum[:rows]).astype(BF16),
            (summed[rows:, 128:] / weight_sum[rows:]).astype(BF16),
        ]
        attended = jnp.concatenate(attended, axis=1)
        out_rows = members * 32
        for lane in range(0, width, 512):
            sides = []
            for start in (lane, width + lane):
                product = jnp.dot(
                    attended,
                    out_all[:, :, pl.ds(start, 512)].reshape(out_rows, 512),
                    preferred_element_type=F32,
                )
                sides.append(product.reshape(slices, 8, 512) * gate[:, pl.ds(start, 512)])
            packed = jnp.concatenate(sides, axis=1)
            partials[p, :, :, pl.ds(lane, 512)] = packed.astype(BF16)

        @pl.when(is_last)
        def _():
            for d in order:
                scatter_copy(p, d, 1).start()

        @pl.when(jnp.logical_not(is_last))
        def _():
            for d in order + [0]:
                scatter_copy(p, d, 0).start()

    def finish_patch(p):
        total = inputs[p].astype(F32) + partials[p, y].astype(F32)
        for d in reversed(order):
            scatter_copy(p, d, 1).wait_recv()
            total = total + arrived[1, p, d].astype(F32)
        finals[p] = total.astype(BF16)
        cfg_copy(p).start()

    def guided_copy(p, device):
        return remote(
            guided_sent.at[p], guided_out, guided_send.at[p], guided_recv, at(device, 0)
        )

    def guide(p):
        cfg_copy(p).wait_recv()
        own, other = finals[p].astype(F32), partner[p].astype(F32)
        first = branch == 0
        own = jnp.where(first, own[:8], own[8:])
        other = jnp.where(first, other[:8], other[8:])
        conditional = jnp.where(first, own, other)
        unconditional = jnp.where(first, other, own)
        guided = unconditional + GUIDANCE_SCALE * (conditional - unconditional)
        return packed_rows(guided).astype(BF16)

    def send_guided(p):
        guided_sent[p] = guide(p)
        guided_copy(p, p).start()

    local_copies[3].wait()
    for lane in range(16):
        lanes = pl.ds(lane % 8 * 128, 128)
        half = pl.ds(lane // 8 * 8, 8)
        row = lambda kind: jnp.broadcast_to(raw_modulation[pl.ds(kind * 16 + lane, 1), :], (8, 128))
        shift[half, lanes] = row(0)
        scale[half, lanes] = 1.0 + row(1)
        gate[:, pl.ds(lane * 128, 128)] = row(2)

    queries[...] = jnp.zeros_like(queries)

    def each_patch(body):
        def step(p, carry):
            body(p)
            return carry

        lax.fori_loop(0, patches, step, 0)

    @pl.when(is_first)
    def _():
        local_copies[-1].wait()
        each_patch(start_patch)

    for step in range(1, middle + 1):
        for item in items:
            if step == middle and item in (2, 3):
                continue
            pl.when(here(item))(functools.partial(land, item, step))
    take_handed(0)
    take_handed(1)
    local_copies[4].wait()
    pl.when(is_first)(lambda: each_patch(project))
    land(2, middle)
    pl.when(here(3))(functools.partial(land, 3, middle))

    @pl.when(is_first)
    def _():
        for slot in range(1, members):
            help_back(slot).wait_recv()

    take_handed(4)
    local_copies[5].wait()

    def tick(p):
        @pl.when(jnp.logical_not(is_first))
        def _():
            project(p)
            pl.when(p < patches - 1)(lambda: start_patch(p + 1))

        attend(p)

        @pl.when(jnp.logical_and(is_last, p > 0))
        def _():
            finish_patch(p - 1)

        @pl.when(jnp.logical_and(is_last, p > 1))
        def _():
            send_guided(p - 2)

    pl.when(jnp.logical_not(is_first))(lambda: start_patch(0))
    each_patch(tick)

    @pl.when(is_last)
    def _():
        finish_patch(patches - 1)
        send_guided(patches - 2)
        guided_out[...] = guide(patches - 1)

    @pl.when(jnp.logical_not(is_last))
    def _():
        guided_copy(0, sections - 1).wait_recv()

    def drain_ring(item):
        for step in range(1, middle + 1):
            for way in ways(item, step):
                hop(item, step, way).wait_send()
                if item not in (2, 3, 5):
                    handed(item, step, way).wait_send()

    for item in items:
        pl.when(here(item))(functools.partial(drain_ring, item))
    pl.when(is_first)(lambda: help_out().wait_send())

    @pl.when(is_last)
    def _():
        drain_ring(5)
        for slot in range(1, members):
            help_back(slot).wait_send()

    def drain(p):
        for d in order:
            gather_copy(p, d).wait_send()

        @pl.when(jnp.logical_not(is_last))
        def _():
            pipe_copy(p).wait_send()
            for d in order + [0]:
                scatter_copy(p, d, 0).wait_send()

        @pl.when(is_last)
        def _():
            cfg_copy(p).wait_send()
            for d in order:
                scatter_copy(p, d, 1).wait_send()

        @pl.when(jnp.logical_and(is_last, p < patches - 1))
        def _():
            guided_copy(p, p).wait_send()

    each_patch(drain)


def local(latent, modulation, qkv_weight, out_weight, norm_gain, stale_kv):
    patches, tok_dev, model_width = latent.shape
    sections = lax.axis_size("pipe")
    slices = 8
    members = lax.axis_size("seq") // slices
    half = model_width // 2
    group_rows = slices * tok_dev
    local_width = stale_kv.shape[7]
    packed = 2 * tok_dev
    latent_packed = (
        latent.reshape(patches, tok_dev, 2, half)
        .transpose(0, 2, 1, 3)
        .reshape(patches, packed, half)
    )
    modulation_rows = modulation.reshape(3 * model_width // 128, 128)
    qkv_piece = qkv_weight[0].T
    qkv_piece = qkv_piece.reshape(2, qkv_piece.shape[0] // 2, model_width)
    out_piece = out_weight[0]
    out_piece = out_piece.reshape(2, out_piece.shape[0] // 2, model_width)
    stale = stale_kv[0, 0].reshape(2, patches, group_rows, local_width)
    dma = pltpu.SemaphoreType.DMA
    vmem = pl.BlockSpec(memory_space=pltpu.VMEM)
    blocks = members * 2
    guided, own_kv = pl.pallas_call(
        functools.partial(kernel, (sections, slices, members, patches)),
        out_shape=(
            jax.ShapeDtypeStruct((packed, half // 2), BF16),
            jax.ShapeDtypeStruct(stale.shape, BF16),
        ),
        in_specs=[pl.BlockSpec(memory_space=pltpu.HBM)] * 6,
        out_specs=(vmem, vmem),
        scratch_shapes=[
            pltpu.VMEM((blocks,) + qkv_piece.shape[1:], BF16),
            pltpu.VMEM((blocks,) + out_piece.shape[1:], BF16),
            pltpu.VMEM((members,) + stale.shape, BF16),
            pltpu.VMEM((members,) + stale.shape[1:], BF16),
            pltpu.VMEM(modulation_rows.shape, F32),
            pltpu.VMEM(norm_gain.shape[1:], F32),
            pltpu.VMEM((packed, half), F32),
            pltpu.VMEM((packed, half), F32),
            pltpu.VMEM((tok_dev, model_width), F32),
            pltpu.VMEM((patches, packed, half), BF16),
            pltpu.VMEM((patches, packed, half), BF16),
            pltpu.VMEM((patches, slices, packed, half), BF16),
            pltpu.VMEM((2, group_rows, half), BF16),
            pltpu.VMEM((patches, 2 * group_rows, local_width), BF16),
            pltpu.VMEM((patches, 2, group_rows, local_width), BF16),
            pltpu.VMEM((patches, slices, packed, half), BF16),
            pltpu.VMEM((2, patches, slices, packed, half), BF16),
            pltpu.VMEM((patches, packed, half), BF16),
            pltpu.VMEM((patches, packed, half), BF16),
            pltpu.VMEM((patches, packed, half // 2), BF16),
            dma((7,)),
            dma((6, 2, 4)),
            dma((6, 2, 4)),
            dma((6, 2, 4)),
            dma((6, 2, 4)),
            dma((members,)),
            dma((members,)),
            dma((patches, slices)),
            dma((patches, slices)),
            dma((patches, slices)),
            dma((2, patches, slices)),
            dma((patches,)),
            dma((patches,)),
            dma((patches,)),
            dma((patches,)),
            dma((patches,)),
            dma(()),
        ],
        compiler_params=pltpu.CompilerParams(
            collective_id=0, has_side_effects=True, vmem_limit_bytes=63 * 2**20 + 2**19
        ),
    )(latent_packed, modulation_rows, qkv_piece, out_piece, norm_gain[0], stale)
    guided = (
        guided.reshape(2, tok_dev, half // 2)
        .transpose(1, 0, 2)
        .reshape(1, tok_dev, half)
    )
    return guided, own_kv.reshape(stale_kv.shape)


def solution(mesh):
    placed = (
        P(None, "seq", None),
        P("pipe", "cfg", None, None),
        P("pipe", None, "seq"),
        P("pipe", "seq", None),
        P("pipe", None, None),
        P("pipe", "cfg", None, None, "seq", None, None, None),
    )
    return jax.shard_map(
        local,
        mesh=mesh,
        in_specs=placed,
        out_specs=(P("pipe", "seq", "cfg"), P("pipe", "cfg", None, None, "seq", None, None, None)),
        check_vma=False,
    )
```

```python
import functools
import math

import jax
import jax.numpy as jnp
from jax import lax
from jax.experimental import pallas as pl
from jax.experimental.pallas import tpu as pltpu
from jax.sharding import PartitionSpec as P

GUIDANCE_SCALE = 6.0
EPSILON = 1e-06
MESH = pl.DeviceIdType.MESH
F32 = jnp.float32
BF16 = jnp.bfloat16
NT = (((1,), (1,)), ((), ()))


def packed_rows(values):
    half = values.shape[-1] // 2
    return jnp.concatenate((values[..., :half], values[..., half:]), axis=-2)


def head_norm(values, gain_row):
    square = jnp.mean(values * values, axis=-1, keepdims=True)
    return values * lax.rsqrt(square + EPSILON) * gain_row


def kernel(
    sizes,
    latent,
    modulation,
    qkv_piece,
    out_piece,
    norm_gain,
    stale,
    guided_out,
    own_kv,
    qkv_all,
    out_all,
    caches,
    helped,
    raw_modulation,
    gains,
    shift,
    scale,
    gate,
    inputs,
    residuals,
    features,
    mixed_left,
    queries,
    fresh,
    partials,
    arrived,
    finals,
    partner,
    guided_sent,
    local_sem,
    z_send,
    z_recv,
    pair_send,
    pair_recv,
    help_send,
    help_recv,
    gather_send,
    gather_recv,
    scatter_send,
    scatter_recv,
    pipe_send,
    pipe_recv,
    cfg_send,
    cfg_recv,
    guided_send,
    guided_recv,
):
    sections, slices, members, patches = sizes
    branch = lax.axis_index("cfg")
    section = lax.axis_index("pipe")
    rank = lax.axis_index("seq")
    y = rank // members
    z = rank % members
    rows = features.shape[1] * 8
    width = features.shape[3]
    middle = members // 2
    is_first = section == 0
    is_last = section == sections - 1

    local_copies = [
        pltpu.make_async_copy(src, dst, local_sem.at[n])
        for n, (src, dst) in enumerate(
            (
                (qkv_piece, qkv_all.at[pl.ds(z * 2, 2)]),
                (stale, caches.at[0]),
                (out_piece, out_all.at[pl.ds(z * 2, 2)]),
                (modulation, raw_modulation),
                (norm_gain, gains),
                (stale, own_kv),
                (latent, inputs),
            )
        )
    ]
    for copy in local_copies[:-1]:
        copy.start()
    pl.when(is_first)(local_copies[-1].start)

    def at_z(index):
        return (branch, section, y * members + index)

    right = at_z((z + 1) % members)
    left = at_z((z + members - 1) % members)
    sibling = (1 - branch, section, rank)

    def at(plane, d):
        return (branch, plane, (y + d) % slices * members + z)

    following = (section + 1) % sections
    barrier = pltpu.get_barrier_semaphore()
    greeted = [right, left, sibling] + [at(section, d) for d in range(1, slices)]
    for d in range(slices):
        greeted += [at(following, d), at((section + sections - 1) % sections, d)]
    greeted += [at((section + d) % sections, 0) for d in range(2, sections - 1)]
    for device in greeted:
        pl.semaphore_signal(barrier, inc=1, device_id=device, device_id_type=MESH)
    pl.semaphore_wait(barrier, len(greeted))

    def remote(src, dst, send, recv, device):
        return pltpu.make_async_remote_copy(
            src_ref=src,
            dst_ref=dst,
            send_sem=send,
            recv_sem=recv,
            device_id=device,
            device_id_type=MESH,
        )

    def block(item, step, way, half, distance):
        if item in (2, 3, 5):
            slot = distance if way == 0 else (members - distance) % members
            return helped.at[slot] if item == 5 else caches.at[slot, item - 2]
        sign = 1 if way else members - 1
        owner = (z + sign * distance) % members
        if item == 4:
            ref = out_all.at[owner * 2 + half]
            return ref if step < middle else ref.at[:, pl.ds(way * 1024, 1024)]
        return qkv_all.at[owner * 2 + half, :, pl.ds(item * 1024, 1024)]

    def ways(item, step):
        return (0, 1) if step < middle or item == 4 else (item % 2,)

    def hop(item, step, way, lands=False):
        here = block(item, step, way, branch, step - 1)
        if item in (2, 3, 5) or lands:
            there = block(item, step, way, branch, step)
        else:
            there = here
        send, recv = z_send.at[item, way, step - 1], z_recv.at[item, way, step - 1]
        return remote(here, there, send, recv, left if way else right)

    def handed(item, step, way, lands=False):
        ref = block(item, step, way, 1 - branch if lands else branch, step)
        send, recv = pair_send.at[item, way, step - 1], pair_recv.at[item, way, step - 1]
        return remote(ref, ref, send, recv, sibling)

    def help_out():
        return remote(
            caches.at[0, 1], helped.at[0], help_send.at[0], help_recv.at[0], at(sections - 1, 0)
        )

    def help_back(slot):
        return remote(
            helped.at[slot], caches.at[slot, 1], help_send.at[slot], help_recv.at[slot], at(0, 0)
        )

    def land(item, step):
        for way in ways(item, step):
            hop(item, step, way, lands=True).wait_recv()
            if step < middle and way in ways(item, step + 1):
                hop(item, step + 1, way).start()
            if item == 5:
                help_back(step if way == 0 else members - step).start()
            elif item not in (2, 3):
                handed(item, step, way).start()

    def take_handed(item):
        for step in range(1, middle + 1):
            for way in ways(item, step):
                handed(item, step, way, lands=True).wait_recv()

    items = (0, 1, 2, 3, 4)
    def here(item):
        return jnp.logical_not(is_first) if item == 3 else section >= 0

    for n in range(3):
        local_copies[n].wait()
    pl.when(is_first)(lambda: help_out().start())

    @pl.when(is_last)
    def _():
        help_out().wait_recv()
        for way in ways(5, 1):
            hop(5, 1, way).start()
        for step in range(1, 3 + 1):
            land(5, step)

    for item in items:
        @pl.when(here(item))
        def _():
            for way in ways(item, 1):
                hop(item, 1, way).start()

    @pl.when(is_last)
    def _():
        for step in range(3 + 1, middle + 1):
            land(5, step)

    order = [4, 3, 5, 2, 6, 1, 7] if slices == 8 else list(range(1, slices))

    def gather_copy(p, d):
        return remote(
            features.at[p, y],
            features.at[p, y],
            gather_send.at[p, d],
            gather_recv.at[p, d],
            at(section, d),
        )

    def gather_landing(p, d):
        return remote(
            features.at[p, y],
            features.at[p, (y + slices - d) % slices],
            gather_send.at[p, d],
            gather_recv.at[p, d],
            at(section, d),
        )

    def scatter_copy(p, d, last):
        return remote(
            partials.at[p, (y + d) % slices],
            arrived.at[last, p, d],
            scatter_send.at[p, d],
            scatter_recv.at[last, p, d],
            at(section if last else following, d),
        )

    def pipe_copy(p):
        return remote(
            inputs.at[p], residuals.at[p], pipe_send.at[p], pipe_recv.at[p], at(following, 0)
        )

    def cfg_copy(p):
        return remote(finals.at[p], partner.at[p], cfg_send.at[p], cfg_recv.at[p], sibling)

    def both(left_rows):
        total = left_rows[:8] + left_rows[8:]
        return jnp.concatenate((total, total), axis=0)

    def start_patch(p):
        @pl.when(jnp.logical_not(is_first))
        def _():
            pipe_copy(p).wait_recv()
            total = residuals[p].astype(F32)
            for d in [0] + order[::-1]:
                scatter_copy(p, d, 0).wait_recv()
                total = total + arrived[0, p, d].astype(F32)
            inputs[p] = total.astype(BF16)

        x = inputs[p].astype(F32)
        count = 2 * width
        center = x - both(jnp.sum(x, axis=1, keepdims=True)) / count
        spread = both(jnp.sum(center * center, axis=1, keepdims=True)) / count
        normed = center * lax.rsqrt(spread + EPSILON)
        features[p, y] = (normed * scale[...] + shift[...]).astype(BF16)
        for d in order:
            gather_copy(p, d).start()
        pl.when(jnp.logical_not(is_last))(lambda: pipe_copy(p).start())

    def project(p):
        for d in order:
            gather_landing(p, d).wait_recv()
        stacked = features[p].astype(F32)
        halves = [
            stacked[:, 8 * side : 8 * side + 8] for side in (0, 1)
        ]
        halves = [half.reshape(rows, width).astype(BF16) for half in halves]
        for head in range(2):
            total = None
            for piece in range(4):
                side, lane = piece // 2, (piece % 2) * 512
                weight = qkv_all[pl.ds(head * members, members), :, pl.ds(piece * 512, 512)]
                product = lax.dot_general(
                    halves[side][:, lane : lane + 512],
                    weight.reshape(members * weight.shape[1], 512),
                    NT,
                    preferred_element_type=F32,
                )
                total = product if total is None else total + product
            lanes = pl.ds(head * 128, 128)
            queries[p, pl.ds(head * rows, rows), lanes] = head_norm(total[:, :128], gains[0:1]).astype(BF16)
            fresh[p, 0, :, lanes] = head_norm(total[:, 128:256], gains[1:2]).astype(BF16)
            fresh[p, 1, :, lanes] = total[:, 256:].astype(BF16)

    def attend(p):
        own_kv[0, p] = fresh[p, 0]
        own_kv[1, p] = fresh[p, 1]
        factor = math.log2(math.e) / math.sqrt(128)
        query = queries[p]
        summed, weight_sum = None, None
        for first in range(0, members, 4):
            blocks = [own_kv if n == 0 else caches.at[n] for n in range(first, first + 4)]
            scores = [
                lax.dot_general(
                    query,
                    block[0].reshape(patches * rows, 256),
                    NT,
                    preferred_element_type=F32,
                )
                for block in blocks
            ]
            for block, score in zip(blocks, scores):
                weights = jnp.exp2(score * factor)
                product = jnp.dot(
                    weights.astype(BF16),
                    block[1].reshape(patches * rows, 256),
                    preferred_element_type=F32,
                )
                summed = product if summed is None else summed + product
                weight_sum = weights if weight_sum is None else weight_sum + weights
        weight_sum = jnp.sum(weight_sum, axis=1, keepdims=True)
        attended = [
            (summed[:rows, :128] / weight_sum[:rows]).astype(BF16),
            (summed[rows:, 128:] / weight_sum[rows:]).astype(BF16),
        ]
        attended = jnp.concatenate(attended, axis=1)
        out_rows = members * 32
        for lane in range(0, width, 1024):
            sides = []
            for start in (lane, width + lane):
                product = jnp.dot(
                    attended,
                    out_all[:, :, pl.ds(start, 1024)].reshape(out_rows, 1024),
                    preferred_element_type=F32,
                )
                sides.append(product.reshape(slices, 8, 1024) * gate[:, pl.ds(start, 1024)])
            packed = jnp.concatenate(sides, axis=1)
            partials[p, :, :, pl.ds(lane, 1024)] = packed.astype(BF16)

        @pl.when(is_last)
        def _():
            for d in order:
                scatter_copy(p, d, 1).start()

        @pl.when(jnp.logical_not(is_last))
        def _():
            for d in order + [0]:
                scatter_copy(p, d, 0).start()

    def finish_patch(p):
        total = inputs[p].astype(F32) + partials[p, y].astype(F32)
        for d in reversed(order):
            scatter_copy(p, d, 1).wait_recv()
            total = total + arrived[1, p, d].astype(F32)
        finals[p] = total.astype(BF16)
        cfg_copy(p).start()

    def guided_copy(p, device):
        return remote(
            guided_sent.at[p], guided_out, guided_send.at[p], guided_recv, at(device, 0)
        )

    def guide(p):
        cfg_copy(p).wait_recv()
        own, other = finals[p].astype(F32), partner[p].astype(F32)
        first = branch == 0
        own = jnp.where(first, own[:8], own[8:])
        other = jnp.where(first, other[:8], other[8:])
        conditional = jnp.where(first, own, other)
        unconditional = jnp.where(first, other, own)
        guided = unconditional + GUIDANCE_SCALE * (conditional - unconditional)
        return packed_rows(guided).astype(BF16)

    def send_guided(p):
        guided_sent[p] = guide(p)
        guided_copy(p, p).start()

    local_copies[3].wait()
    for lane in range(16):
        lanes = pl.ds(lane % 8 * 128, 128)
        half = pl.ds(lane // 8 * 8, 8)
        row = lambda kind: jnp.broadcast_to(raw_modulation[pl.ds(kind * 16 + lane, 1), :], (8, 128))
        shift[half, lanes] = row(0)
        scale[half, lanes] = 1.0 + row(1)
        gate[:, pl.ds(lane * 128, 128)] = row(2)

    queries[...] = jnp.zeros_like(queries)

    def each_patch(body):
        def step(p, carry):
            body(p)
            return carry

        lax.fori_loop(0, patches, step, 0)

    @pl.when(is_first)
    def _():
        local_copies[-1].wait()
        each_patch(start_patch)

    for step in range(1, middle + 1):
        for item in items:
            if step == middle and item in (2, 3):
                continue
            pl.when(here(item))(functools.partial(land, item, step))
    take_handed(0)
    take_handed(1)
    local_copies[4].wait()
    pl.when(is_first)(lambda: each_patch(project))
    land(2, middle)
    pl.when(here(3))(functools.partial(land, 3, middle))

    @pl.when(is_first)
    def _():
        for slot in range(1, members):
            help_back(slot).wait_recv()

    take_handed(4)
    local_copies[5].wait()

    def tick(p):
        @pl.when(jnp.logical_not(is_first))
        def _():
            project(p)
            pl.when(p < patches - 1)(lambda: start_patch(p + 1))

        attend(p)

        @pl.when(jnp.logical_and(is_last, p > 0))
        def _():
            finish_patch(p - 1)

        @pl.when(jnp.logical_and(is_last, p > 1))
        def _():
            send_guided(p - 2)

    pl.when(jnp.logical_not(is_first))(lambda: start_patch(0))
    each_patch(tick)

    @pl.when(is_last)
    def _():
        finish_patch(patches - 1)
        send_guided(patches - 2)
        guided_out[...] = guide(patches - 1)

    @pl.when(jnp.logical_not(is_last))
    def _():
        guided_copy(0, sections - 1).wait_recv()

    def drain_ring(item):
        for step in range(1, middle + 1):
            for way in ways(item, step):
                hop(item, step, way).wait_send()
                if item not in (2, 3, 5):
                    handed(item, step, way).wait_send()

    for item in items:
        pl.when(here(item))(functools.partial(drain_ring, item))
    pl.when(is_first)(lambda: help_out().wait_send())

    @pl.when(is_last)
    def _():
        drain_ring(5)
        for slot in range(1, members):
            help_back(slot).wait_send()

    def drain(p):
        for d in order:
            gather_copy(p, d).wait_send()

        @pl.when(jnp.logical_not(is_last))
        def _():
            pipe_copy(p).wait_send()
            for d in order + [0]:
                scatter_copy(p, d, 0).wait_send()

        @pl.when(is_last)
        def _():
            cfg_copy(p).wait_send()
            for d in order:
                scatter_copy(p, d, 1).wait_send()

        @pl.when(jnp.logical_and(is_last, p < patches - 1))
        def _():
            guided_copy(p, p).wait_send()

    each_patch(drain)


def local(latent, modulation, qkv_weight, out_weight, norm_gain, stale_kv):
    patches, tok_dev, model_width = latent.shape
    sections = lax.axis_size("pipe")
    slices = 8
    members = lax.axis_size("seq") // slices
    half = model_width // 2
    group_rows = slices * tok_dev
    local_width = stale_kv.shape[7]
    packed = 2 * tok_dev
    latent_packed = (
        latent.reshape(patches, tok_dev, 2, half)
        .transpose(0, 2, 1, 3)
        .reshape(patches, packed, half)
    )
    modulation_rows = modulation.reshape(3 * model_width // 128, 128)
    qkv_piece = qkv_weight[0].T
    qkv_piece = qkv_piece.reshape(2, qkv_piece.shape[0] // 2, model_width)
    out_piece = out_weight[0]
    out_piece = out_piece.reshape(2, out_piece.shape[0] // 2, model_width)
    stale = stale_kv[0, 0].reshape(2, patches, group_rows, local_width)
    dma = pltpu.SemaphoreType.DMA
    vmem = pl.BlockSpec(memory_space=pltpu.VMEM)
    blocks = members * 2
    guided, own_kv = pl.pallas_call(
        functools.partial(kernel, (sections, slices, members, patches)),
        out_shape=(
            jax.ShapeDtypeStruct((packed, half // 2), BF16),
            jax.ShapeDtypeStruct(stale.shape, BF16),
        ),
        in_specs=[pl.BlockSpec(memory_space=pltpu.HBM)] * 6,
        out_specs=(vmem, vmem),
        scratch_shapes=[
            pltpu.VMEM((blocks,) + qkv_piece.shape[1:], BF16),
            pltpu.VMEM((blocks,) + out_piece.shape[1:], BF16),
            pltpu.VMEM((members,) + stale.shape, BF16),
            pltpu.VMEM((members,) + stale.shape[1:], BF16),
            pltpu.VMEM(modulation_rows.shape, F32),
            pltpu.VMEM(norm_gain.shape[1:], F32),
            pltpu.VMEM((packed, half), F32),
            pltpu.VMEM((packed, half), F32),
            pltpu.VMEM((tok_dev, model_width), F32),
            pltpu.VMEM((patches, packed, half), BF16),
            pltpu.VMEM((patches, packed, half), BF16),
            pltpu.VMEM((patches, slices, packed, half), BF16),
            pltpu.VMEM((2, group_rows, half), BF16),
            pltpu.VMEM((patches, 2 * group_rows, local_width), BF16),
            pltpu.VMEM((patches, 2, group_rows, local_width), BF16),
            pltpu.VMEM((patches, slices, packed, half), BF16),
            pltpu.VMEM((2, patches, slices, packed, half), BF16),
            pltpu.VMEM((patches, packed, half), BF16),
            pltpu.VMEM((patches, packed, half), BF16),
            pltpu.VMEM((patches, packed, half // 2), BF16),
            dma((7,)),
            dma((6, 2, 4)),
            dma((6, 2, 4)),
            dma((6, 2, 4)),
            dma((6, 2, 4)),
            dma((members,)),
            dma((members,)),
            dma((patches, slices)),
            dma((patches, slices)),
            dma((patches, slices)),
            dma((2, patches, slices)),
            dma((patches,)),
            dma((patches,)),
            dma((patches,)),
            dma((patches,)),
            dma((patches,)),
            dma(()),
        ],
        compiler_params=pltpu.CompilerParams(
            collective_id=0, has_side_effects=True, vmem_limit_bytes=63 * 2**20 + 2**19
        ),
    )(latent_packed, modulation_rows, qkv_piece, out_piece, norm_gain[0], stale)
    guided = (
        guided.reshape(2, tok_dev, half // 2)
        .transpose(1, 0, 2)
        .reshape(1, tok_dev, half)
    )
    return guided, own_kv.reshape(stale_kv.shape)


def solution(mesh):
    placed = (
        P(None, "seq", None),
        P("pipe", "cfg", None, None),
        P("pipe", None, "seq"),
        P("pipe", "seq", None),
        P("pipe", None, None),
        P("pipe", "cfg", None, None, "seq", None, None, None),
    )
    return jax.shard_map(
        local,
        mesh=mesh,
        in_specs=placed,
        out_specs=(P("pipe", "seq", "cfg"), P("pipe", "cfg", None, None, "seq", None, None, None)),
        check_vma=False,
    )
```

```python
import functools
import math

import jax
import jax.numpy as jnp
from jax import lax
from jax.experimental import pallas as pl
from jax.experimental.pallas import tpu as pltpu
from jax.sharding import PartitionSpec as P

GUIDANCE_SCALE = 6.0
EPSILON = 1e-06
MESH = pl.DeviceIdType.MESH
F32 = jnp.float32
BF16 = jnp.bfloat16
NT = (((1,), (1,)), ((), ()))


def packed_rows(values):
    half = values.shape[-1] // 2
    return jnp.concatenate((values[..., :half], values[..., half:]), axis=-2)


def head_norm(values, gain_row):
    square = jnp.mean(values * values, axis=-1, keepdims=True)
    return values * lax.rsqrt(square + EPSILON) * gain_row


def kernel(
    sizes,
    latent,
    modulation,
    qkv_piece,
    out_piece,
    norm_gain,
    stale,
    guided_out,
    own_kv,
    qkv_all,
    out_all,
    caches,
    helped,
    raw_modulation,
    gains,
    shift,
    scale,
    gate,
    inputs,
    residuals,
    features,
    mixed_left,
    queries,
    fresh,
    partials,
    arrived,
    finals,
    partner,
    guided_sent,
    local_sem,
    z_send,
    z_recv,
    pair_send,
    pair_recv,
    help_send,
    help_recv,
    gather_send,
    gather_recv,
    scatter_send,
    scatter_recv,
    pipe_send,
    pipe_recv,
    cfg_send,
    cfg_recv,
    guided_send,
    guided_recv,
):
    sections, slices, members, patches = sizes
    branch = lax.axis_index("cfg")
    section = lax.axis_index("pipe")
    rank = lax.axis_index("seq")
    y = rank // members
    z = rank % members
    rows = features.shape[1] * 8
    width = features.shape[3]
    middle = members // 2
    is_first = section == 0
    is_last = section == sections - 1

    local_copies = [
        pltpu.make_async_copy(src, dst, local_sem.at[n])
        for n, (src, dst) in enumerate(
            (
                (qkv_piece, qkv_all.at[pl.ds(z * 2, 2)]),
                (stale, caches.at[0]),
                (out_piece, out_all.at[pl.ds(z * 2, 2)]),
                (modulation, raw_modulation),
                (norm_gain, gains),
                (stale, own_kv),
                (latent, inputs),
            )
        )
    ]
    for copy in local_copies[:-1]:
        copy.start()
    pl.when(is_first)(local_copies[-1].start)

    def at_z(index):
        return (branch, section, y * members + index)

    right = at_z((z + 1) % members)
    left = at_z((z + members - 1) % members)
    sibling = (1 - branch, section, rank)

    def at(plane, d):
        return (branch, plane, (y + d) % slices * members + z)

    following = (section + 1) % sections
    barrier = pltpu.get_barrier_semaphore()
    greeted = [right, left, sibling] + [at(section, d) for d in range(1, slices)]
    for d in range(slices):
        greeted += [at(following, d), at((section + sections - 1) % sections, d)]
    greeted += [at((section + d) % sections, 0) for d in range(2, sections - 1)]
    for device in greeted:
        pl.semaphore_signal(barrier, inc=1, device_id=device, device_id_type=MESH)
    pl.semaphore_wait(barrier, len(greeted))

    def remote(src, dst, send, recv, device):
        return pltpu.make_async_remote_copy(
            src_ref=src,
            dst_ref=dst,
            send_sem=send,
            recv_sem=recv,
            device_id=device,
            device_id_type=MESH,
        )

    def block(item, step, way, half, distance):
        if item in (2, 3, 5):
            slot = distance if way == 0 else (members - distance) % members
            return helped.at[slot] if item == 5 else caches.at[slot, item - 2]
        sign = 1 if way else members - 1
        owner = (z + sign * distance) % members
        if item == 4:
            ref = out_all.at[owner * 2 + half]
            return ref if step < middle else ref.at[:, pl.ds(way * 1024, 1024)]
        return qkv_all.at[owner * 2 + half, :, pl.ds(item * 1024, 1024)]

    def ways(item, step):
        return (0, 1) if step < middle or item == 4 else (item % 2,)

    def hop(item, step, way, lands=False):
        here = block(item, step, way, branch, step - 1)
        if item in (2, 3, 5) or lands:
            there = block(item, step, way, branch, step)
        else:
            there = here
        send, recv = z_send.at[item, way, step - 1], z_recv.at[item, way, step - 1]
        return remote(here, there, send, recv, left if way else right)

    def handed(item, step, way, lands=False):
        ref = block(item, step, way, 1 - branch if lands else branch, step)
        send, recv = pair_send.at[item, way, step - 1], pair_recv.at[item, way, step - 1]
        return remote(ref, ref, send, recv, sibling)

    def help_out():
        return remote(
            caches.at[0, 1], helped.at[0], help_send.at[0], help_recv.at[0], at(sections - 1, 0)
        )

    def help_back(slot):
        return remote(
            helped.at[slot], caches.at[slot, 1], help_send.at[slot], help_recv.at[slot], at(0, 0)
        )

    def land(item, step):
        for way in ways(item, step):
            hop(item, step, way, lands=True).wait_recv()
            if step < middle and way in ways(item, step + 1):
                hop(item, step + 1, way).start()
            if item == 5:
                help_back(step if way == 0 else members - step).start()
            elif item not in (2, 3):
                handed(item, step, way).start()

    def take_handed(item):
        for step in range(1, middle + 1):
            for way in ways(item, step):
                handed(item, step, way, lands=True).wait_recv()

    items = (0, 1, 2, 3, 4)
    def here(item):
        return jnp.logical_not(is_first) if item == 3 else section >= 0

    for n in range(3):
        local_copies[n].wait()
    pl.when(is_first)(lambda: help_out().start())

    @pl.when(is_last)
    def _():
        help_out().wait_recv()
        for way in ways(5, 1):
            hop(5, 1, way).start()
        for step in range(1, 3 + 1):
            land(5, step)

    for item in items:
        @pl.when(here(item))
        def _():
            for way in ways(item, 1):
                hop(item, 1, way).start()

    @pl.when(is_last)
    def _():
        for step in range(3 + 1, middle + 1):
            land(5, step)

    order = [4, 3, 5, 2, 6, 1, 7] if slices == 8 else list(range(1, slices))

    def gather_copy(p, d):
        return remote(
            features.at[p, y],
            features.at[p, y],
            gather_send.at[p, d],
            gather_recv.at[p, d],
            at(section, d),
        )

    def gather_landing(p, d):
        return remote(
            features.at[p, y],
            features.at[p, (y + slices - d) % slices],
            gather_send.at[p, d],
            gather_recv.at[p, d],
            at(section, d),
        )

    def scatter_copy(p, d, last):
        return remote(
            partials.at[p, (y + d) % slices],
            arrived.at[last, p, d],
            scatter_send.at[p, d],
            scatter_recv.at[last, p, d],
            at(section if last else following, d),
        )

    def pipe_copy(p):
        return remote(
            inputs.at[p], residuals.at[p], pipe_send.at[p], pipe_recv.at[p], at(following, 0)
        )

    def cfg_copy(p):
        return remote(finals.at[p], partner.at[p], cfg_send.at[p], cfg_recv.at[p], sibling)

    def both(left_rows):
        total = left_rows[:8] + left_rows[8:]
        return jnp.concatenate((total, total), axis=0)

    def start_patch(p):
        @pl.when(jnp.logical_not(is_first))
        def _():
            pipe_copy(p).wait_recv()
            total = residuals[p].astype(F32)
            for d in [0] + order[::-1]:
                scatter_copy(p, d, 0).wait_recv()
                total = total + arrived[0, p, d].astype(F32)
            inputs[p] = total.astype(BF16)

        x = inputs[p].astype(F32)
        count = 2 * width
        center = x - both(jnp.sum(x, axis=1, keepdims=True)) / count
        spread = both(jnp.sum(center * center, axis=1, keepdims=True)) / count
        normed = center * lax.rsqrt(spread + EPSILON)
        features[p, y] = (normed * scale[...] + shift[...]).astype(BF16)
        for d in order:
            gather_copy(p, d).start()
        pl.when(jnp.logical_not(is_last))(lambda: pipe_copy(p).start())

    def project(p):
        for d in order:
            gather_landing(p, d).wait_recv()
        stacked = features[p].astype(F32)
        halves = [
            stacked[:, 8 * side : 8 * side + 8] for side in (0, 1)
        ]
        halves = [half.reshape(rows, width).astype(BF16) for half in halves]
        for head in range(2):
            total = None
            for piece in range(4):
                side, lane = piece // 2, (piece % 2) * 512
                weight = qkv_all[pl.ds(head * members, members), :, pl.ds(piece * 512, 512)]
                product = lax.dot_general(
                    halves[side][:, lane : lane + 512],
                    weight.reshape(members * weight.shape[1], 512),
                    NT,
                    preferred_element_type=F32,
                )
                total = product if total is None else total + product
            lanes = pl.ds(head * 128, 128)
            queries[p, pl.ds(head * rows, rows), lanes] = head_norm(total[:, :128], gains[0:1]).astype(BF16)
            fresh[p, 0, :, lanes] = head_norm(total[:, 128:256], gains[1:2]).astype(BF16)
            fresh[p, 1, :, lanes] = total[:, 256:].astype(BF16)

    def attend(p):
        own_kv[0, p] = fresh[p, 0]
        own_kv[1, p] = fresh[p, 1]
        factor = math.log2(math.e) / math.sqrt(128)
        query = queries[p]
        summed, weight_sum = None, None
        for first in range(0, members, 2):
            blocks = [own_kv if n == 0 else caches.at[n] for n in range(first, first + 2)]
            scores = [
                lax.dot_general(
                    query,
                    block[0].reshape(patches * rows, 256),
                    NT,
                    preferred_element_type=F32,
                )
                for block in blocks
            ]
            for block, score in zip(blocks, scores):
                weights = jnp.exp2(score * factor)
                product = jnp.dot(
                    weights.astype(BF16),
                    block[1].reshape(patches * rows, 256),
                    preferred_element_type=F32,
                )
                summed = product if summed is None else summed + product
                weight_sum = weights if weight_sum is None else weight_sum + weights
        weight_sum = jnp.sum(weight_sum, axis=1, keepdims=True)
        attended = [
            (summed[:rows, :128] / weight_sum[:rows]).astype(BF16),
            (summed[rows:, 128:] / weight_sum[rows:]).astype(BF16),
        ]
        attended = jnp.concatenate(attended, axis=1)
        out_rows = members * 32
        for lane in range(0, width, 1024):
            sides = []
            for start in (lane, width + lane):
                product = jnp.dot(
                    attended,
                    out_all[:, :, pl.ds(start, 1024)].reshape(out_rows, 1024),
                    preferred_element_type=F32,
                )
                sides.append(product.reshape(slices, 8, 1024) * gate[:, pl.ds(start, 1024)])
            packed = jnp.concatenate(sides, axis=1)
            partials[p, :, :, pl.ds(lane, 1024)] = packed.astype(BF16)

        @pl.when(is_last)
        def _():
            for d in order:
                scatter_copy(p, d, 1).start()

        @pl.when(jnp.logical_not(is_last))
        def _():
            for d in order + [0]:
                scatter_copy(p, d, 0).start()

    def finish_patch(p):
        total = inputs[p].astype(F32) + partials[p, y].astype(F32)
        for d in reversed(order):
            scatter_copy(p, d, 1).wait_recv()
            total = total + arrived[1, p, d].astype(F32)
        finals[p] = total.astype(BF16)
        cfg_copy(p).start()

    def guided_copy(p, device):
        return remote(
            guided_sent.at[p], guided_out, guided_send.at[p], guided_recv, at(device, 0)
        )

    def guide(p):
        cfg_copy(p).wait_recv()
        own, other = finals[p].astype(F32), partner[p].astype(F32)
        first = branch == 0
        own = jnp.where(first, own[:8], own[8:])
        other = jnp.where(first, other[:8], other[8:])
        conditional = jnp.where(first, own, other)
        unconditional = jnp.where(first, other, own)
        guided = unconditional + GUIDANCE_SCALE * (conditional - unconditional)
        return packed_rows(guided).astype(BF16)

    def send_guided(p):
        guided_sent[p] = guide(p)
        guided_copy(p, p).start()

    local_copies[3].wait()
    for lane in range(16):
        lanes = pl.ds(lane % 8 * 128, 128)
        half = pl.ds(lane // 8 * 8, 8)
        row = lambda kind: jnp.broadcast_to(raw_modulation[pl.ds(kind * 16 + lane, 1), :], (8, 128))
        shift[half, lanes] = row(0)
        scale[half, lanes] = 1.0 + row(1)
        gate[:, pl.ds(lane * 128, 128)] = row(2)

    queries[...] = jnp.zeros_like(queries)

    def each_patch(body):
        def step(p, carry):
            body(p)
            return carry

        lax.fori_loop(0, patches, step, 0)

    @pl.when(is_first)
    def _():
        local_copies[-1].wait()
        each_patch(start_patch)

    for step in range(1, middle + 1):
        for item in items:
            if step == middle and item in (2, 3):
                continue
            pl.when(here(item))(functools.partial(land, item, step))
    take_handed(0)
    take_handed(1)
    local_copies[4].wait()
    pl.when(is_first)(lambda: each_patch(project))
    land(2, middle)
    pl.when(here(3))(functools.partial(land, 3, middle))

    @pl.when(is_first)
    def _():
        for slot in range(1, members):
            help_back(slot).wait_recv()

    take_handed(4)
    local_copies[5].wait()

    def tick(p):
        @pl.when(jnp.logical_not(is_first))
        def _():
            project(p)
            pl.when(p < patches - 1)(lambda: start_patch(p + 1))

        attend(p)

        @pl.when(jnp.logical_and(is_last, p > 0))
        def _():
            finish_patch(p - 1)

        @pl.when(jnp.logical_and(is_last, p > 1))
        def _():
            send_guided(p - 2)

    pl.when(jnp.logical_not(is_first))(lambda: start_patch(0))
    each_patch(tick)

    @pl.when(is_last)
    def _():
        finish_patch(patches - 1)
        send_guided(patches - 2)
        guided_out[...] = guide(patches - 1)

    @pl.when(jnp.logical_not(is_last))
    def _():
        guided_copy(0, sections - 1).wait_recv()

    def drain_ring(item):
        for step in range(1, middle + 1):
            for way in ways(item, step):
                hop(item, step, way).wait_send()
                if item not in (2, 3, 5):
                    handed(item, step, way).wait_send()

    for item in items:
        pl.when(here(item))(functools.partial(drain_ring, item))
    pl.when(is_first)(lambda: help_out().wait_send())

    @pl.when(is_last)
    def _():
        drain_ring(5)
        for slot in range(1, members):
            help_back(slot).wait_send()

    def drain(p):
        for d in order:
            gather_copy(p, d).wait_send()

        @pl.when(jnp.logical_not(is_last))
        def _():
            pipe_copy(p).wait_send()
            for d in order + [0]:
                scatter_copy(p, d, 0).wait_send()

        @pl.when(is_last)
        def _():
            cfg_copy(p).wait_send()
            for d in order:
                scatter_copy(p, d, 1).wait_send()

        @pl.when(jnp.logical_and(is_last, p < patches - 1))
        def _():
            guided_copy(p, p).wait_send()

    each_patch(drain)


def local(latent, modulation, qkv_weight, out_weight, norm_gain, stale_kv):
    patches, tok_dev, model_width = latent.shape
    sections = lax.axis_size("pipe")
    slices = 8
    members = lax.axis_size("seq") // slices
    half = model_width // 2
    group_rows = slices * tok_dev
    local_width = stale_kv.shape[7]
    packed = 2 * tok_dev
    latent_packed = (
        latent.reshape(patches, tok_dev, 2, half)
        .transpose(0, 2, 1, 3)
        .reshape(patches, packed, half)
    )
    modulation_rows = modulation.reshape(3 * model_width // 128, 128)
    qkv_piece = qkv_weight[0].T
    qkv_piece = qkv_piece.reshape(2, qkv_piece.shape[0] // 2, model_width)
    out_piece = out_weight[0]
    out_piece = out_piece.reshape(2, out_piece.shape[0] // 2, model_width)
    stale = stale_kv[0, 0].reshape(2, patches, group_rows, local_width)
    dma = pltpu.SemaphoreType.DMA
    vmem = pl.BlockSpec(memory_space=pltpu.VMEM)
    blocks = members * 2
    guided, own_kv = pl.pallas_call(
        functools.partial(kernel, (sections, slices, members, patches)),
        out_shape=(
            jax.ShapeDtypeStruct((packed, half // 2), BF16),
            jax.ShapeDtypeStruct(stale.shape, BF16),
        ),
        in_specs=[pl.BlockSpec(memory_space=pltpu.HBM)] * 6,
        out_specs=(vmem, vmem),
        scratch_shapes=[
            pltpu.VMEM((blocks,) + qkv_piece.shape[1:], BF16),
            pltpu.VMEM((blocks,) + out_piece.shape[1:], BF16),
            pltpu.VMEM((members,) + stale.shape, BF16),
            pltpu.VMEM((members,) + stale.shape[1:], BF16),
            pltpu.VMEM(modulation_rows.shape, F32),
            pltpu.VMEM(norm_gain.shape[1:], F32),
            pltpu.VMEM((packed, half), F32),
            pltpu.VMEM((packed, half), F32),
            pltpu.VMEM((tok_dev, model_width), F32),
            pltpu.VMEM((patches, packed, half), BF16),
            pltpu.VMEM((patches, packed, half), BF16),
            pltpu.VMEM((patches, slices, packed, half), BF16),
            pltpu.VMEM((2, group_rows, half), BF16),
            pltpu.VMEM((patches, 2 * group_rows, local_width), BF16),
            pltpu.VMEM((patches, 2, group_rows, local_width), BF16),
            pltpu.VMEM((patches, slices, packed, half), BF16),
            pltpu.VMEM((2, patches, slices, packed, half), BF16),
            pltpu.VMEM((patches, packed, half), BF16),
            pltpu.VMEM((patches, packed, half), BF16),
            pltpu.VMEM((patches, packed, half // 2), BF16),
            dma((7,)),
            dma((6, 2, 4)),
            dma((6, 2, 4)),
            dma((6, 2, 4)),
            dma((6, 2, 4)),
            dma((members,)),
            dma((members,)),
            dma((patches, slices)),
            dma((patches, slices)),
            dma((patches, slices)),
            dma((2, patches, slices)),
            dma((patches,)),
            dma((patches,)),
            dma((patches,)),
            dma((patches,)),
            dma((patches,)),
            dma(()),
        ],
        compiler_params=pltpu.CompilerParams(
            collective_id=0, has_side_effects=True, vmem_limit_bytes=63 * 2**20 + 2**19
        ),
    )(latent_packed, modulation_rows, qkv_piece, out_piece, norm_gain[0], stale)
    guided = (
        guided.reshape(2, tok_dev, half // 2)
        .transpose(1, 0, 2)
        .reshape(1, tok_dev, half)
    )
    return guided, own_kv.reshape(stale_kv.shape)


def solution(mesh):
    placed = (
        P(None, "seq", None),
        P("pipe", "cfg", None, None),
        P("pipe", None, "seq"),
        P("pipe", "seq", None),
        P("pipe", None, None),
        P("pipe", "cfg", None, None, "seq", None, None, None),
    )
    return jax.shard_map(
        local,
        mesh=mesh,
        in_specs=placed,
        out_specs=(P("pipe", "seq", "cfg"), P("pipe", "cfg", None, None, "seq", None, None, None)),
        check_vma=False,
    )
```
